512 devices in a mesh: grp: 16 (over z_lo, core), blk: 32 (over y, x, z_hi).
Axes of the slice: x: 4, y: 4, z: 16 (z_hi: 2, z_lo: 8; z = z_hi * 8 + z_lo), core: 2. Of those that a mesh axis runs over, the one named last changes fastest.
Arguments:
- three_centre: bfloat16 [128, 32, 8, 128, 128], P('grp', 'blk'), may hold values from -0.1875 to 0.1875
- occupied_coefficients: bfloat16 [4096, 1024], P('blk', 'grp'), may hold values from -6 to 6
- paired_blocks: int32 [32, 8], P('blk'), may hold values from 0 to 31, as said below
- stored_counts: int32 [32], P('blk'), may hold values from 2 to 8, as said below
Outputs:
- exchange_diagonal: float32 [32, 128, 128], P('blk', 'grp')
- exchange_next: float32 [32, 128, 128], P('blk', 'grp')
The draws below stay inside these ranges and needn't reach their ends.
Inputs may be any that keep to these rules, and one draw needn't show every extreme that they name: `paired_blocks`: row m names block m in its first slot, block (m - 1) mod 32 in its second, and 6 other distinct blocks after them. Block m uses its first stored_counts[m] slots; later slots of paired_blocks and three_centre are ignored. Some block uses all 8 slots and some block only two.
All inputs are finite; a program needn't handle non-finite values.
Results may differ from the reference program's by a relative error of at most 0.0031.
Values may be sent and summed in bfloat16 or wider, within the bound.
A program may use at most 64 MiB of HBM per device.

```python
import math
import jax
import jax.numpy as jnp
from jax import lax

BS = 128
NOCC = 1024
SLOTS = 8
NBLOCKS = 32
NAUX = 128
NBAS = 4096


def draw_paired_blocks(key, part):
    key = jax.random.fold_in(key, 11)
    row_ids = jnp.arange(NBLOCKS, dtype=jnp.int32)
    row_keys = jax.random.split(key, NBLOCKS)
    shuffled = jax.vmap(lambda row_key: jax.random.permutation(row_key, NBLOCKS - 2))(row_keys)
    others = (row_ids[:, None] + 1 + shuffled[:, :SLOTS - 2]) % NBLOCKS
    before = (row_ids[:, None] + NBLOCKS - 1) % NBLOCKS
    return jnp.concatenate([row_ids[:, None], before, others], axis=1).astype(jnp.int32)


def draw_stored_counts(key, part):
    key = jax.random.fold_in(key, 23)
    first_key, second_key, third_key = jax.random.split(key, 3)
    first_draw = jax.random.randint(first_key, (NBLOCKS,), 1, SLOTS + 1)
    second_draw = jax.random.randint(second_key, (NBLOCKS,), 1, SLOTS + 1)
    counts = jnp.maximum(2, first_draw * second_draw // SLOTS)
    picked = jax.random.permutation(third_key, NBLOCKS)
    counts = counts.at[picked[0]].set(SLOTS)
    counts = counts.at[picked[1]].set(2)
    return counts.astype(jnp.int32)


def levels(stream_key, shape, pieces, low, top_value):
    factor_of = 1.0
    for axis_at, shards_of in pieces:
        steps = jax.random.uniform(jax.random.fold_in(jax.random.fold_in(stream_key, 6), axis_at), (shards_of,), jnp.float32, low / len(pieces), top_value / len(pieces))
        factor_of = factor_of * jnp.repeat(jnp.exp(steps), shape[axis_at] // shards_of).reshape((-1,) + (1,) * (len(shape) - 1 - axis_at))
    return factor_of


def normal_values(key, dims, width, reach, shards=(), kind=jnp.bfloat16):
    loudness = levels(key, dims, shards, -0.22, 0.18) if shards else 1.0
    entries = jax.random.normal(key, dims, jnp.float32) * width * loudness
    return jnp.minimum(jnp.maximum(entries, -reach), reach).astype(kind)


def setup_inputs(seed: int = 0) -> dict:
    splits = jax.random.split(jax.random.key(seed), 5)
    three_centre = normal_values(splits[0], (NAUX, NBLOCKS, SLOTS, BS, BS), (BS * SLOTS) ** -0.5, 0.1875, ((0, 16), (1, 32)))
    occupied_coefficients = normal_values(splits[1], (NBAS, NOCC), 1.0, 6.0, ((0, 32), (1, 16)))
    paired_blocks = draw_paired_blocks(jax.random.fold_in(splits[4], 71), 0)
    stored_counts = draw_stored_counts(jax.random.fold_in(splits[4], 71), 0)
    return dict(three_centre=three_centre, occupied_coefficients=occupied_coefficients, paired_blocks=paired_blocks, stored_counts=stored_counts)


def half_transform(block_id, three_centre, occupied_coefficients, paired_blocks, stored_counts):
    tensor = lax.dynamic_index_in_dim(three_centre, block_id, 1, keepdims=False)
    running = jnp.zeros((NAUX, BS, NOCC), jnp.float32)
    for slot_id in range(SLOTS):
        row_start = (paired_blocks[block_id, slot_id] * BS).astype(jnp.int32)
        coef_rows = lax.dynamic_slice_in_dim(occupied_coefficients, row_start, BS, 0)
        product = jnp.einsum('pab,bi->pai', tensor[:, slot_id].astype(jnp.float32), coef_rows.astype(jnp.float32))
        running = running + jnp.where(slot_id < stored_counts[block_id], product, jnp.zeros_like(product))
    return running.astype(jnp.bfloat16)

def contract(row_slab, column_slab):
    factor = 1.0 / math.sqrt(NAUX * NOCC)
    return jnp.einsum('pai,pci->ac', row_slab.astype(jnp.float32), column_slab.astype(jnp.float32)) * factor

def reference(three_centre, occupied_coefficients, paired_blocks, stored_counts):

    def make_slab(block_id):
        return half_transform(block_id, three_centre, occupied_coefficients, paired_blocks, stored_counts)
    first_slab = make_slab(jnp.int32(0))

    def advance(previous, block_id):
        current = make_slab(block_id)
        return (current, (contract(current, current), contract(previous, current)))
    final_slab, (diagonals, crossings) = lax.scan(advance, first_slab, jnp.arange(1, NBLOCKS, dtype=jnp.int32))
    exchange_diagonal = jnp.concatenate([contract(first_slab, first_slab)[None], diagonals], axis=0)
    exchange_next = jnp.concatenate([crossings, contract(final_slab, first_slab)[None]], axis=0)
    return (exchange_diagonal, exchange_next)
```

```python
import functools
import math

import jax
import jax.numpy as jnp
from jax import lax
from jax.experimental import pallas as pl
from jax.experimental.pallas import tpu as pltpu
from jax.sharding import PartitionSpec as P

MESH = pl.DeviceIdType.MESH
F32 = jnp.float32
BF16 = jnp.bfloat16
NX, NY, NZ, HALF, CORES = 4, 4, 16, 8, 2
RINGS = NX * NY


def nt(a, b):
    return lax.dot_general(a, b, (((1,), (1,)), ((), ())), preferred_element_type=F32)


def at_device(ring, z, core):
    return {
        "grp": lax.rem(z, HALF) * CORES + core,
        "blk": ring * 2 + z // HALF,
    }


def kernel(factor, tab_ref, c_ref, t_ref, diag_ref, next_ref,
           ct, c_all, t_own, t_cross, t_side, mid, csel, h_own, h_side, gram, side,
           stage_a, stage_b, stage_c, parts, tab_cross, tab_side, tabs,
           ct_send, c1_recv, cx_send, cx_recv, cy_send, cy_recv,
           cross_send, mid_recv, fwd_send, cross_recv, side_send, side_recv,
           tab_send, tab_cross_recv, tab_side_recv, own_sem, smem_sem,
           part_send, part_recv):
    naux, slots, bs = t_ref.shape[0], t_ref.shape[2], t_ref.shape[3]
    cols = c_ref.shape[1]
    nblk = RINGS * 2
    quarter = naux // 2

    g = lax.axis_index("grp")
    b = lax.axis_index("blk")
    zlo, core = g // CORES, lax.rem(g, CORES)
    ring, hi = b // 2, lax.rem(b, 2)
    y, x = ring // NX, lax.rem(ring, NX)
    z = hi * HALF + zlo
    takes = core == hi
    gives = core != hi

    def remote(src, dst, ssem, rsem, dev):
        return pltpu.make_async_remote_copy(
            src_ref=src, dst_ref=dst, send_sem=ssem, recv_sem=rsem,
            device_id=dev, device_id_type=MESH)

    piece = c_ref[...].astype(F32)
    piece = jnp.concatenate([piece, jnp.zeros((bs, bs - cols), F32)], axis=1)
    ct[...] = piece.T[:cols].astype(BF16)

    def c1_copy(zt):
        return remote(ct, c_all.at[b, pl.ds(pl.multiple_of(g * cols, cols), cols)],
                      ct_send.at[zt], c1_recv, at_device(ring, zt, zt // HALF))

    def c1_local():
        return pltpu.make_async_copy(
            ct, c_all.at[b, pl.ds(pl.multiple_of(g * cols, cols), cols)], c1_recv)

    def c1_start(zt, carry):
        own = jnp.logical_and(zt == z, takes)

        @pl.when(own)
        def _():
            c1_local().start()

        @pl.when(jnp.logical_not(own))
        def _():
            c1_copy(zt).start()
        return carry

    lax.fori_loop(0, NZ, c1_start, 0)

    up = lax.rem(z + 4, NZ)
    down = lax.rem(z + NZ - 4, NZ)

    def cross_copy(k, upward):
        dest = up if upward else down
        p = k if upward else quarter + k
        return remote(t_ref.at[p, 0], mid.at[k], cross_send.at[p], mid_recv.at[k],
                      at_device(ring, dest, core))

    def tab_copy():
        return remote(tab_ref, tab_cross, tab_send, tab_cross_recv,
                      at_device(ring, lax.rem(z + HALF, NZ), core))

    @pl.when(gives)
    def _():
        for k in range(quarter):
            cross_copy(k, True).start()
            cross_copy(k, False).start()
        tab_copy().start()

    sender_below = (down // HALF) != core
    onward = jnp.where(sender_below, up, down)
    first = jnp.where(sender_below, 0, quarter)

    def fwd_copy(k):
        return remote(mid.at[k], t_cross.at[first + k], fwd_send.at[k], cross_recv.at[first + k],
                      at_device(ring, onward, core))

    def forward(k):
        pltpu.make_async_copy(mid.at[k], mid.at[k], mid_recv.at[k]).wait()
        fwd_copy(k).start()

    step = jnp.where(hi == 0, RINGS - 1, 1)
    side_ring = lax.rem(ring + step, RINGS)

    def side_copy():
        return remote(t_ref.at[:, 0], t_side, side_send.at[0], side_recv, at_device(side_ring, z, core))

    def side_tab_copy():
        return remote(tab_ref, tab_side, side_send.at[1], tab_side_recv, at_device(side_ring, z, core))

    def own_copy():
        return pltpu.make_async_copy(t_ref.at[:, 0], t_own, own_sem)

    def ring_at(xx, yy):
        return lax.rem(yy, NY) * NX + lax.rem(xx, NX)

    def cx_copy(i):
        r = [ring, ring, ring_at(x + 3, y), ring_at(x + 1, y)][i]
        dest = [ring_at(x + 1, y), ring_at(x + 3, y)][i % 2]
        part = c_all.at[pl.ds(2 * r, 2)] if i < 2 else c_all.at[pl.ds(2 * r + (i - 2), 1)]
        return remote(part, part, cx_send.at[i], cx_recv.at[i], at_device(dest, z, core))

    def cx_wait(i):
        n = 2 if i < 2 else 1
        part = c_all.at[pl.ds(0, n)]
        pltpu.make_async_copy(part, part, cx_recv.at[i]).wait()

    row = 2 * NX

    def cy_copy(i):
        r = [y, y, lax.rem(y + 3, NY), lax.rem(y + 1, NY)][i]
        dest = [ring_at(x, y + 1), ring_at(x, y + 3)][i % 2]
        if i < 2:
            part = c_all.at[pl.ds(row * r, row)]
        else:
            part = c_all.at[pl.ds(row * r + (i - 2) * (row // 2), row // 2)]
        return remote(part, part, cy_send.at[i], cy_recv.at[i], at_device(dest, z, core))

    def cy_wait(i):
        n = row if i < 2 else row // 2
        part = c_all.at[pl.ds(0, n)]
        pltpu.make_async_copy(part, part, cy_recv.at[i]).wait()

    def choose(ti):
        count = tabs[ti, 0, slots]
        for s in range(slots):
            pair = jnp.where(s < count, tabs[ti, 0, s], nblk)
            csel[:, s * bs:(s + 1) * bs] = c_all[pair]

    def half(t_buf, p):
        lhs = jnp.concatenate([t_buf[p, s] for s in range(slots)], axis=1)
        return nt(lhs, csel[...]).astype(BF16)

    def part_copies(gd):
        ring_c = jnp.where(hi == 0, ring, lax.rem(ring + RINGS - 1, RINGS))
        to_a = {"grp": gd, "blk": 2 * ring}
        to_b = {"grp": gd, "blk": 2 * ring + 1}
        to_c = {"grp": gd, "blk": 2 * ring_c + 1}
        return (remote(stage_a.at[gd], parts.at[g], part_send.at[0, gd], part_recv, to_a),
                remote(stage_b.at[gd], parts.at[g, 0], part_send.at[1, gd], part_recv, to_b),
                remote(stage_c.at[gd], parts.at[g, 1], part_send.at[2, gd], part_recv, to_c))

    @pl.when(takes)
    def _():
        side_copy().start()
        side_tab_copy().start()
        own_copy().start()
        c_all[nblk] = jnp.zeros(c_all.shape[1:], BF16)
        gram[...] = jnp.zeros_like(gram)
        side[...] = jnp.zeros_like(side)
        here = c_all.at[pl.ds(0, 2)]
        pltpu.make_async_copy(here, here, c1_recv).wait()
        cx_copy(0).start()
        cx_copy(1).start()
        cx_wait(0)
        cx_copy(2).start()
        cx_wait(1)
        cx_copy(3).start()
        forward(0)
        cx_wait(2)
        cx_wait(3)
        cy_copy(0).start()
        cy_copy(1).start()
        forward(1)
        cy_wait(0)
        cy_copy(2).start()
        cy_wait(1)
        cy_copy(3).start()
        forward(2)
        cy_wait(2)
        cy_wait(3)

        pltpu.make_async_copy(tab_cross, tab_cross, tab_cross_recv).wait()
        pltpu.make_async_copy(tab_side, tab_side, tab_side_recv).wait()
        fetch = [pltpu.make_async_copy(v, tabs.at[i], smem_sem.at[i])
                 for i, v in enumerate((tab_ref, tab_side, tab_cross))]
        for f in fetch:
            f.start()
        for f in fetch:
            f.wait()

        own_copy().wait()
        choose(0)

        def own_step(p, carry):
            h_own[p] = half(t_own, p)
            return carry
        lax.fori_loop(0, naux, own_step, 0)
        forward(3)
        pltpu.make_async_copy(t_side, t_side, side_recv).wait()
        choose(1)

        def side_step(p, carry):
            h_side[p] = half(t_side, p)
            return carry
        lax.fori_loop(0, naux, side_step, 0)
        choose(2)

        def cross_step(j, carry):
            p = lax.rem(j, 2) * quarter + j // 2
            arrived = t_cross.at[p]
            pltpu.make_async_copy(arrived, arrived, cross_recv.at[p]).wait()
            h_cross = half(t_cross, p)
            both = jnp.concatenate([h_own[p], h_cross], axis=0)
            gram[...] += nt(both, both)
            side[...] += nt(h_cross, h_side[p])
            return carry
        lax.fori_loop(0, naux, cross_step, 0)

        def rows(block):
            return block.reshape(stage_b.shape)

        @pl.when(hi == 0)
        def _():
            stage_a[:, 0] = rows(gram[:bs, :bs])
            stage_a[:, 1] = rows(gram[:bs, bs:])
            stage_b[...] = rows(gram[bs:, bs:])
            stage_c[...] = rows(side[...])

        @pl.when(hi == 1)
        def _():
            stage_a[:, 0] = rows(gram[bs:, bs:])
            stage_a[:, 1] = rows(gram[bs:, :bs])
            stage_b[...] = rows(gram[:bs, :bs])
            stage_c[...] = rows(side[...].T)

        def part_start(gd, carry):
            a, bb, c = part_copies(gd)
            mine = gd == g

            @pl.when(jnp.logical_and(mine, hi == 0))
            def _():
                pltpu.make_async_copy(stage_a.at[gd], parts.at[g], part_recv).start()

            @pl.when(jnp.logical_not(jnp.logical_and(mine, hi == 0)))
            def _():
                a.start()

            @pl.when(jnp.logical_and(mine, hi == 1))
            def _():
                pltpu.make_async_copy(stage_b.at[gd], parts.at[g, 0], part_recv).start()

            @pl.when(jnp.logical_not(jnp.logical_and(mine, hi == 1)))
            def _():
                bb.start()
            c.start()
            return carry
        lax.fori_loop(0, HALF * CORES, part_start, 0)

    @pl.when(gives)
    def _():
        for k in range(quarter):
            forward(k)

    pltpu.make_async_copy(parts, parts, part_recv).wait()
    diag_ref[0] = jnp.sum(parts[:, 0], axis=0) * factor
    next_ref[0] = jnp.sum(parts[:, 1], axis=0) * factor

    def c1_done(zt, carry):
        @pl.when(jnp.logical_not(jnp.logical_and(zt == z, takes)))
        def _():
            c1_copy(zt).wait_send()
        return carry
    lax.fori_loop(0, NZ, c1_done, 0)
    for k in range(quarter):
        fwd_copy(k).wait_send()

    @pl.when(gives)
    def _():
        for k in range(quarter):
            cross_copy(k, True).wait_send()
            cross_copy(k, False).wait_send()
        tab_copy().wait_send()

    @pl.when(takes)
    def _():
        side_copy().wait_send()
        side_tab_copy().wait_send()
        for i in range(4):
            cx_copy(i).wait_send()
            cy_copy(i).wait_send()

        def part_done(gd, carry):
            a, bb, c = part_copies(gd)
            mine = gd == g

            @pl.when(jnp.logical_not(jnp.logical_and(mine, hi == 0)))
            def _():
                a.wait_send()

            @pl.when(jnp.logical_not(jnp.logical_and(mine, hi == 1)))
            def _():
                bb.wait_send()
            c.wait_send()
            return carry
        lax.fori_loop(0, HALF * CORES, part_done, 0)


def body(three_centre, occupied_coefficients, paired_blocks, stored_counts):
    naux, _, slots, bs, _ = three_centre.shape
    groups = HALF * CORES
    nocc = occupied_coefficients.shape[1] * groups
    nblk = RINGS * 2
    factor = 1.0 / math.sqrt(naux * groups * nocc)
    tab = jnp.concatenate([paired_blocks[0], stored_counts])
    tab = jnp.broadcast_to(jnp.pad(tab, (0, 128 - tab.shape[0]))[None], (8, 128))
    rows = bs // groups
    dma = pltpu.SemaphoreType.DMA
    vmem = pl.BlockSpec(memory_space=pltpu.VMEM)
    slab = (naux, slots, bs, bs)
    return pl.pallas_call(
        functools.partial(kernel, factor),
        out_shape=[jax.ShapeDtypeStruct((1, rows, bs), F32)] * 2,
        in_specs=[vmem, vmem, pl.BlockSpec(memory_space=pl.ANY)],
        out_specs=[vmem, vmem],
        scratch_shapes=[
            pltpu.VMEM((occupied_coefficients.shape[1], bs), BF16),
            pltpu.VMEM((nblk + 1, nocc, bs), BF16),
            pltpu.VMEM(slab, BF16),
            pltpu.VMEM(slab, BF16),
            pltpu.VMEM(slab, BF16),
            pltpu.VMEM((naux // 2, slots, bs, bs), BF16),
            pltpu.VMEM((nocc, slots * bs), BF16),
            pltpu.VMEM((naux, bs, nocc), BF16),
            pltpu.VMEM((naux, bs, nocc), BF16),
            pltpu.VMEM((2 * bs, 2 * bs), F32),
            pltpu.VMEM((bs, bs), F32),
            pltpu.VMEM((groups, 2, rows, bs), F32),
            pltpu.VMEM((groups, rows, bs), F32),
            pltpu.VMEM((groups, rows, bs), F32),
            pltpu.VMEM((groups, 2, rows, bs), F32),
            pltpu.VMEM((8, 128), jnp.int32),
            pltpu.VMEM((8, 128), jnp.int32),
            pltpu.SMEM((3, 8, 128), jnp.int32),
            dma((NZ,)), dma, dma((4,)), dma((4,)), dma((4,)), dma((4,)),
            dma((naux,)), dma((naux // 2,)), dma((naux // 2,)), dma((naux,)), dma((2,)), dma,
            dma, dma, dma, dma, dma((3,)),
            dma((3, groups)), dma,
        ],
        compiler_params=pltpu.CompilerParams(
            has_side_effects=True, vmem_limit_bytes=48 * 1024 * 1024),
        cost_estimate=pl.CostEstimate(flops=8 * 10**9, bytes_accessed=6 * 2**20, transcendentals=0),
    )(tab, occupied_coefficients, three_centre)


def solution(mesh):
    placed = (P("grp", "blk", None, None, None), P("blk", "grp"), P("blk", None), P("blk"))
    return jax.shard_map(
        body,
        mesh=mesh,
        in_specs=placed,
        out_specs=(P("blk", "grp", None), P("blk", "grp", None)),
        check_vma=False,
    )
```

```python
import functools
import math

import jax
import jax.numpy as jnp
from jax import lax
from jax.experimental import pallas as pl
from jax.experimental.pallas import tpu as pltpu
from jax.sharding import PartitionSpec as P

MESH = pl.DeviceIdType.MESH
F32 = jnp.float32
BF16 = jnp.bfloat16
NX, NY, NZ, HALF, CORES = 4, 4, 16, 8, 2
RINGS = NX * NY


def nt(a, b):
    return lax.dot_general(a, b, (((1,), (1,)), ((), ())), preferred_element_type=F32)


def at_device(ring, z, core):
    return {
        "grp": lax.rem(z, HALF) * CORES + core,
        "blk": ring * 2 + z // HALF,
    }


def kernel(factor, pairs_ref, count_ref, ct_ref, t_ref, diag_ref, next_ref,
           joint, c_all, t_own, t_cross, t_side, mid, csel, h_own, h_side, gram, side,
           stage_a, stage_b, stage_c, parts, total, tab, tab_cross, tab_side, tabs,
           give_send, give_recv, c1_send, c1_recv, plane_send, plane_recv,
           cross_send, mid_recv, fwd_send, cross_recv, side_send, side_recv,
           tab_send, tab_recv, own_sem, smem_sem, part_send, part_recv, total_send, total_recv, ready):
    naux, slots, bs = t_ref.shape[0], t_ref.shape[2], t_ref.shape[3]
    cols = ct_ref.shape[0]
    quarter = naux // 2

    g = lax.axis_index("grp")
    b = lax.axis_index("blk")
    zlo, core = g // CORES, lax.rem(g, CORES)
    ring, hi = b // 2, lax.rem(b, 2)
    y, x = ring // NX, lax.rem(ring, NX)
    z = hi * HALF + zlo
    takes = core == hi
    gives = core != hi

    def remote(src, dst, ssem, rsem, dev):
        return pltpu.make_async_remote_copy(
            src_ref=src, dst_ref=dst, send_sem=ssem, recv_sem=rsem,
            device_id=dev, device_id_type=MESH)

    def arrived(ref, sem):
        pltpu.make_async_copy(ref, ref, sem).wait()

    def ring_at(xx, yy):
        return lax.rem(yy, NY) * NX + lax.rem(xx, NX)

    def taker(zz):
        return at_device(ring, zz, zz // HALF)

    def giver(zz):
        return at_device(ring, zz, 1 - zz // HALF)

    up4, down4 = lax.rem(z + 4, NZ), lax.rem(z + NZ - 4, NZ)
    up1, down1 = lax.rem(z + 1, NZ), lax.rem(z + NZ - 1, NZ)
    up2, down2 = lax.rem(z + 2, NZ), lax.rem(z + NZ - 2, NZ)
    across = lax.rem(z + HALF, NZ)
    partner = {"grp": zlo * CORES + 1 - core, "blk": b}
    step = jnp.where(hi == 0, RINGS - 1, 1)
    side_dest = at_device(lax.rem(ring + step, RINGS), z, core)
    side_source = at_device(lax.rem(ring + RINGS - step, RINGS), z, core)
    east, west = at_device(ring_at(x + 1, y), z, core), at_device(ring_at(x + 3, y), z, core)
    north, south = at_device(ring_at(x, y + 1), z, core), at_device(ring_at(x, y + 3), z, core)

    barrier = pltpu.get_barrier_semaphore()

    def greet(dev):
        pl.semaphore_signal(barrier, inc=1, device_id=dev, device_id_type=MESH)

    def cross_copy(k, upward):
        p = k if upward else quarter + k
        return remote(t_ref.at[p, 0], mid.at[p], cross_send.at[p], mid_recv.at[p],
                      giver(up4 if upward else down4))

    def fwd_copy(k, upward):
        p = k if upward else quarter + k
        return remote(mid.at[p], t_cross.at[p], fwd_send.at[p], cross_recv.at[p],
                      taker(up4 if upward else down4))

    rows = total.shape[1] // 2

    def total_copy():
        return remote(total.at[:, pl.ds(pl.multiple_of((1 - hi) * rows, rows), rows)],
                      parts.at[0, :, pl.ds(0, rows)], total_send, total_recv, partner)

    def piece_at(cc):
        return joint.at[pl.ds(pl.multiple_of(cc * cols, cols), cols)]

    def give_copy():
        return remote(ct_ref, piece_at(core), give_send, give_recv, partner)

    @pl.when(gives)
    def _():
        greet(giver(up4))
        greet(giver(down4))
        greet(taker(up4))
        greet(taker(down4))
        greet(partner)
        pl.semaphore_wait(barrier, 2)
        for k in range(quarter):
            cross_copy(k, True).start()
            cross_copy(k, False).start()
        pl.semaphore_wait(ready, 3)
        give_copy().start()
        for k in range(quarter):
            for upward in (True, False):
                p = k if upward else quarter + k
                arrived(mid.at[p], mid_recv.at[p])
                fwd_copy(k, upward).start()
        give_copy().wait_send()
        for k in range(quarter):
            for upward in (True, False):
                cross_copy(k, upward).wait_send()
                fwd_copy(k, upward).wait_send()
        got = parts.at[0, :, pl.ds(0, rows)]
        arrived(got, total_recv)
        diag_ref[0] = got[0]
        next_ref[0] = got[1]

    def side_copy():
        return remote(t_ref.at[:, 0], t_side, side_send, side_recv, side_dest)

    def tab_copy(i):
        return remote(tab, (tab_side, tab_cross)[i], tab_send.at[i], tab_recv.at[i],
                      (side_dest, taker(across))[i])

    def own_copy():
        return pltpu.make_async_copy(t_ref.at[:, 0], t_own, own_sem)

    def c1_part(zz):
        return c_all.at[y, x, zz // HALF, lax.rem(zz, HALF)]

    def c1_copy(o, hop, upward):
        part = c1_part(lax.rem(z + NZ - o if upward else z + o, NZ))
        i = 0 if upward else 1
        dest = (up1 if upward else down1) if hop == 1 else (up2 if upward else down2)
        return remote(part, part, c1_send.at[i, o + hop], c1_recv.at[i, o + hop], taker(dest))

    def c1_wait(o, upward):
        arrived(c1_part(0), c1_recv.at[0 if upward else 1, o])

    c1_steps = [[(0, 2), (0, 1)], [(2, 2), (1, 2)], [(4, 2), (3, 2)], [(6, 2), (5, 2)]]
    c1_moves = [(st, o, hop, upward) for st, moves in enumerate(c1_steps) for o, hop in moves
                for upward in (True, False) if upward or o + hop < NZ // 2]

    half_rows = HALF // 2

    def plane_part(path, stage, i):
        i_rows = pl.ds(path * half_rows, half_rows)
        along_x = path == stage
        if stage == 0:
            if i < 2:
                return c_all.at[y, x, :, i_rows]
            o = lax.rem((x if along_x else y) + (3 if i == 2 else 1), NX)
            return c_all.at[y if along_x else o, o if along_x else x, pl.ds(i - 2, 1), i_rows]
        if i < 2:
            return c_all.at[pl.ds(0, NY), x, :, i_rows] if along_x else c_all.at[y, :, :, i_rows]
        o = lax.rem((x if along_x else y) + (3 if i == 2 else 1), NX)
        two = pl.ds(2 * (i - 2), 2)
        return c_all.at[two, o, :, i_rows] if along_x else c_all.at[o, two, :, i_rows]

    def plane_copy(path, stage, i):
        part = plane_part(path, stage, i)
        dev = ([east, west] if path == stage else [north, south])[i % 2]
        return remote(part, part, plane_send.at[path, stage, i], plane_recv.at[path, stage, i], dev)

    def plane_wait(path, stage, i):
        arrived(plane_part(path, stage, i), plane_recv.at[path, stage, i])

    def choose(pair_of, count):
        for s in range(slots):
            pair = pair_of(s)
            live = s < count
            block = c_all[jnp.where(live, pair // (2 * NX), NY),
                          jnp.where(live, lax.rem(pair // 2, NX), 0),
                          jnp.where(live, lax.rem(pair, 2), 0)]
            for q in range(HALF):
                csel[s * bs:(s + 1) * bs, q * bs:(q + 1) * bs] = block[q]

    def half(t_buf, k):
        lhs = jnp.concatenate(
            [jnp.concatenate([t_buf[p, s] for s in range(slots)], axis=1) for p in (k, quarter + k)], axis=0)
        both = jnp.dot(lhs, csel[...], preferred_element_type=F32).astype(BF16)
        return both[:bs], both[bs:]

    ring_c = jnp.where(hi == 0, ring, lax.rem(ring + RINGS - 1, RINGS))

    def part_a(i):
        return remote(stage_a.at[i], parts.at[g], part_send.at[0], part_recv,
                      {"grp": 2 * i, "blk": 2 * ring})

    def part_b(i):
        return remote(stage_b.at[i], parts.at[g, 0], part_send.at[1], part_recv,
                      {"grp": 2 * i + 1, "blk": 2 * ring + 1})

    def part_c(i):
        return remote(stage_c.at[i], parts.at[g, 1], part_send.at[2], part_recv,
                      {"grp": 2 * i + 1, "blk": 2 * ring_c + 1})

    @pl.when(takes)
    def _():
        for dev in [taker(up1), taker(down1), taker(up2), taker(down2), taker(across), east, west, north, south, side_source]:
            greet(dev)
        own_copy().start()
        piece_at(core)[...] = ct_ref[...]
        lane = lax.broadcasted_iota(jnp.int32, tab.shape, 1)
        table = jnp.where(lane == slots, count_ref[0, 0], 0)
        for s in range(slots):
            table = jnp.where(lane == s, pairs_ref[0, s], table)
        tab[...] = table
        pl.semaphore_wait(barrier, 13)
        for dev in (giver(up4), giver(down4), partner):
            pl.semaphore_signal(ready, inc=1, device_id=dev, device_id_type=MESH)
        tab_copy(0).start()
        tab_copy(1).start()
        side_copy().start()
        c_all[NY, 0, 0] = jnp.zeros(c_all.shape[3:], BF16)
        gram[...] = jnp.zeros_like(gram)
        side[...] = jnp.zeros_like(side)
        arrived(piece_at(1 - core), give_recv)
        c_all[y, x, hi, zlo] = joint[...].astype(F32).T.astype(BF16)
        for st in range(len(c1_steps)):
            for m in c1_moves:
                if m[0] == st:
                    c1_copy(*m[1:]).start()
            for m in c1_moves:
                if m[0] == st:
                    c1_wait(m[1] + m[2], m[3])
        for stage in range(2):
            for path in range(2):
                plane_copy(path, stage, 0).start()
                plane_copy(path, stage, 1).start()
            for i in range(2):
                for path in range(2):
                    plane_wait(path, stage, i)
                    plane_copy(path, stage, 2 + i).start()
            for path in range(2):
                plane_wait(path, stage, 2)
                plane_wait(path, stage, 3)
        arrived(tab_side, tab_recv.at[0])
        arrived(tab_cross, tab_recv.at[1])
        fetch = [pltpu.make_async_copy(v, tabs.at[i], smem_sem.at[i])
                 for i, v in enumerate((tab_side, tab_cross))]
        for f in fetch:
            f.start()
        for f in fetch:
            f.wait()
        own_copy().wait()
        arrived(t_side, side_recv)

        choose(lambda s: pairs_ref[0, s], count_ref[0, 0])

        def own_step(k, carry):
            h_own[k], h_own[quarter + k] = half(t_own, k)
            return carry
        lax.fori_loop(0, quarter, own_step, 0)
        choose(lambda s: tabs[0, 0, s], tabs[0, 0, slots])

        def side_step(k, carry):
            h_side[k], h_side[quarter + k] = half(t_side, k)
            return carry
        lax.fori_loop(0, quarter, side_step, 0)
        choose(lambda s: tabs[1, 0, s], tabs[1, 0, slots])

        def cross_step(k, carry):
            for p in (k, quarter + k):
                arrived(t_cross.at[p], cross_recv.at[p])
            for p, h_cross in zip((k, quarter + k), half(t_cross, k)):
                both = jnp.concatenate([h_own[p], h_cross], axis=0)
                gram[...] += nt(both, both)
                side[...] += nt(h_cross, h_side[p])
            return carry
        lax.fori_loop(0, quarter, cross_step, 0)

        def cut(block):
            return block.reshape(stage_b.shape)

        @pl.when(hi == 0)
        def _():
            stage_a[:, 0] = cut(gram[:bs, :bs])
            stage_a[:, 1] = cut(gram[:bs, bs:])
            stage_b[...] = cut(gram[bs:, bs:])
            stage_c[...] = cut(side[...])

        @pl.when(hi == 1)
        def _():
            stage_a[:, 0] = cut(gram[bs:, bs:])
            stage_a[:, 1] = cut(gram[bs:, :bs])
            stage_b[...] = cut(gram[:bs, :bs])
            stage_c[...] = cut(side[...].T)

        for i in range(HALF):
            away_a = jnp.logical_or(zlo != i, hi == 1)
            away_b = jnp.logical_or(zlo != i, hi == 0)

            @pl.when(away_a)
            def _():
                part_a(i).start()

            @pl.when(jnp.logical_not(away_a))
            def _():
                pltpu.make_async_copy(stage_a.at[i], parts.at[g], part_recv).start()

            @pl.when(away_b)
            def _():
                part_b(i).start()

            @pl.when(jnp.logical_not(away_b))
            def _():
                pltpu.make_async_copy(stage_b.at[i], parts.at[g, 0], part_recv).start()
            part_c(i).start()

        arrived(parts, part_recv)
        total[...] = jnp.sum(parts[...], axis=0) * factor
        total_copy().start()
        mine = total[:, pl.ds(pl.multiple_of(hi * rows, rows), rows)]
        diag_ref[0] = mine[0]
        next_ref[0] = mine[1]

        total_copy().wait_send()
        tab_copy(0).wait_send()
        tab_copy(1).wait_send()
        side_copy().wait_send()
        for m in c1_moves:
            c1_copy(*m[1:]).wait_send()
        for path in range(2):
            for stage in range(2):
                for i in range(4):
                    plane_copy(path, stage, i).wait_send()

        @pl.when(hi == 0)
        def _():
            arrived(parts.at[pl.ds(0, HALF - 1)], part_send.at[0])
            arrived(parts.at[pl.ds(0, HALF // 2)], part_send.at[1])

        @pl.when(hi == 1)
        def _():
            arrived(parts.at[pl.ds(0, HALF)], part_send.at[0])
            arrived(parts.at[pl.ds(0, HALF - 1), 0], part_send.at[1])
        arrived(parts.at[pl.ds(0, HALF // 2)], part_send.at[2])


def body(three_centre, occupied_coefficients, paired_blocks, stored_counts):
    naux, _, slots, bs, _ = three_centre.shape
    groups = HALF * CORES
    cols = occupied_coefficients.shape[1]
    nocc = cols * groups
    factor = 1.0 / math.sqrt(naux * groups * nocc)
    rows = bs // groups
    dma = pltpu.SemaphoreType.DMA
    vmem = pl.BlockSpec(memory_space=pltpu.VMEM)
    smem = pl.BlockSpec(memory_space=pltpu.SMEM)
    slab = (naux, slots, bs, bs)
    return pl.pallas_call(
        functools.partial(kernel, factor),
        out_shape=[jax.ShapeDtypeStruct((1, rows, bs), F32)] * 2,
        in_specs=[smem, smem, vmem, pl.BlockSpec(memory_space=pl.ANY)],
        out_specs=[vmem, vmem],
        scratch_shapes=[
            pltpu.VMEM((2 * cols, bs), BF16),
            pltpu.VMEM((NY + 1, NX, 2, HALF, bs, bs), BF16),
            pltpu.VMEM(slab, BF16),
            pltpu.VMEM(slab, BF16),
            pltpu.VMEM(slab, BF16),
            pltpu.VMEM(slab, BF16),
            pltpu.VMEM((slots * bs, nocc), BF16),
            pltpu.VMEM((naux, bs, nocc), BF16),
            pltpu.VMEM((naux, bs, nocc), BF16),
            pltpu.VMEM((2 * bs, 2 * bs), F32),
            pltpu.VMEM((bs, bs), F32),
            pltpu.VMEM((HALF, 2, 2 * rows, bs), F32),
            pltpu.VMEM((HALF, 2 * rows, bs), F32),
            pltpu.VMEM((HALF, 2 * rows, bs), F32),
            pltpu.VMEM((groups, 2, 2 * rows, bs), F32),
            pltpu.VMEM((2, 2 * rows, bs), F32),
            pltpu.VMEM((8, 128), jnp.int32),
            pltpu.VMEM((8, 128), jnp.int32),
            pltpu.VMEM((8, 128), jnp.int32),
            pltpu.SMEM((2, 8, 128), jnp.int32),
            dma, dma, dma((2, NZ // 2 + 1)), dma((2, NZ // 2 + 1)), dma((2, 2, 4)), dma((2, 2, 4)),
            dma((naux,)), dma((naux,)), dma((naux,)), dma((naux,)), dma, dma,
            dma((2,)), dma((2,)), dma, dma((2,)), dma((3,)), dma, dma, dma,
            pltpu.SemaphoreType.REGULAR,
        ],
        compiler_params=pltpu.CompilerParams(
            collective_id=0, has_side_effects=True, vmem_limit_bytes=60 * 1024 * 1024),
        cost_estimate=pl.CostEstimate(flops=8 * 10**9, bytes_accessed=6 * 2**20, transcendentals=0),
    )(paired_blocks, stored_counts[None], occupied_coefficients.T, three_centre)


def solution(mesh):
    placed = (P("grp", "blk", None, None, None), P("blk", "grp"), P("blk", None), P("blk"))
    return jax.shard_map(
        body,
        mesh=mesh,
        in_specs=placed,
        out_specs=(P("blk", "grp", None), P("blk", "grp", None)),
        check_vma=False,
    )
```

```python
import functools
import math

import jax
import jax.numpy as jnp
from jax import lax
from jax.experimental import pallas as pl
from jax.experimental.pallas import tpu as pltpu
from jax.sharding import PartitionSpec as P

MESH = pl.DeviceIdType.MESH
F32 = jnp.float32
BF16 = jnp.bfloat16
NX, NY, NZ, HALF, CORES = 4, 4, 16, 8, 2
RINGS = NX * NY
STILL, ROOM = 4, 20


def nt(a, b):
    return lax.dot_general(a, b, (((1,), (1,)), ((), ())), preferred_element_type=F32)


def at_device(ring, z, core):
    return {
        "grp": lax.rem(z, HALF) * CORES + core,
        "blk": ring * 2 + z // HALF,
    }


def kernel(factor, low, room, pairs_ref, count_ref, ct_ref, t_ref, diag_ref, next_ref, over_ref,
           spread, packed, mid_packed, got_packed, strips, counts, other, over, counts_s, other_s, starts,
           spread_send, spread_recv, counts_send, counts_recv, other_send, other_recv, over_send, over_recv,
           pack_send, pack_mid, pack_fwd, pack_recv, high_send, high_recv, count_sem,
           joint, c_all, t_own, t_cross, t_side, mid, csel, h_own, h_side, gram, side,
           stage_a, stage_b, stage_c, parts, total, tab, tab_cross, tab_side, tabs,
           beside_send, beside_recv, give_send, give_recv, c1_send, c1_recv, plane_send, plane_recv,
           cross_send, mid_recv, fwd_send, cross_recv, side_send, side_recv,
           tab_send, tab_recv, own_sem, smem_sem, part_send, part_recv, total_send, total_recv, ready):
    naux, slots, bs = t_ref.shape[0], t_ref.shape[2], t_ref.shape[3]
    cols = ct_ref.shape[0]
    quarter = naux // 2
    high = slots - low
    per = RINGS // naux
    strip = bs // per

    g = lax.axis_index("grp")
    b = lax.axis_index("blk")
    zlo, core = g // CORES, lax.rem(g, CORES)
    ring, hi = b // 2, lax.rem(b, 2)
    y, x = ring // NX, lax.rem(ring, NX)
    z = hi * HALF + zlo
    takes = core == hi
    gives = core != hi

    def remote(src, dst, ssem, rsem, dev):
        return pltpu.make_async_remote_copy(
            src_ref=src, dst_ref=dst, send_sem=ssem, recv_sem=rsem,
            device_id=dev, device_id_type=MESH)

    def arrived(ref, sem):
        pltpu.make_async_copy(ref, ref, sem).wait()

    def ring_at(xx, yy):
        return lax.rem(yy, NY) * NX + lax.rem(xx, NX)

    def taker(zz):
        return at_device(ring, zz, zz // HALF)

    def giver(zz):
        return at_device(ring, zz, 1 - zz // HALF)

    up4, down4 = lax.rem(z + 4, NZ), lax.rem(z + NZ - 4, NZ)
    beside = z + 1 - 2 * lax.rem(z, 2)
    up2, down2 = lax.rem(z + 2, NZ), lax.rem(z + NZ - 2, NZ)
    across = lax.rem(z + HALF, NZ)
    partner = {"grp": zlo * CORES + 1 - core, "blk": b}
    step = jnp.where(hi == 0, RINGS - 1, 1)
    side_dest = at_device(lax.rem(ring + step, RINGS), z, core)
    side_source = at_device(lax.rem(ring + RINGS - step, RINGS), z, core)
    east, west = at_device(ring_at(x + 1, y), z, core), at_device(ring_at(x + 3, y), z, core)
    north, south = at_device(ring_at(x, y + 1), z, core), at_device(ring_at(x, y + 3), z, core)

    barrier = pltpu.get_barrier_semaphore()

    def greet(dev):
        pl.semaphore_signal(barrier, inc=1, device_id=dev, device_id_type=MESH)

    def cross_copy(k, upward):
        p = k if upward else quarter + k
        return remote(t_ref.at[p, 0, pl.ds(0, low)], mid.at[p], cross_send.at[p], mid_recv.at[p],
                      giver(up4 if upward else down4))

    def fwd_copy(k, upward):
        p = k if upward else quarter + k
        return remote(mid.at[p], t_cross.at[p, pl.ds(0, low)], fwd_send.at[p], cross_recv.at[p],
                      taker(up4 if upward else down4))

    rows = total.shape[1] // 2

    def total_copy():
        return remote(total.at[:, pl.ds(pl.multiple_of((1 - hi) * rows, rows), rows)],
                      parts.at[0, :, pl.ds(0, rows)], total_send, total_recv, partner)

    def piece_at(cc):
        return joint.at[pl.ds(pl.multiple_of(cc * cols, cols), cols)]

    def give_copy():
        return remote(ct_ref, piece_at(core), give_send, give_recv, partner)

    lane = lax.broadcasted_iota(jnp.int32, tab.shape, 1)
    table = jnp.where(lane == slots, count_ref[0, 0], 0)
    for s in range(slots):
        table = jnp.where(lane == s, pairs_ref[0, s], table)
    tab[...] = table

    def strip_of(t, p, part):
        return t.at[p, pl.ds(low, high), pl.ds(pl.multiple_of(part * strip, strip), strip)]

    def spread_copy(r):
        return remote(strip_of(t_ref.at[:, 0], r // per, lax.rem(r, per)), spread.at[ring],
                      spread_send, spread_recv, at_device(r, z, core))

    def counts_copy(r):
        return remote(over, counts.at[ring], counts_send, counts_recv, at_device(r, z, core))

    def other_copy():
        return remote(tab_cross, other, other_send, other_recv, giver(across))

    def over_copy():
        return remote(over_ref, over, over_send, over_recv, partner)

    def pack_copy(upward):
        some = pl.ds(0 if upward else room // 2, room // 2)
        i = 0 if upward else 1
        return remote(packed.at[some], mid_packed.at[some], pack_send.at[i], pack_mid.at[i],
                      giver(up4 if upward else down4))

    def pack_fwd_copy(upward):
        some = pl.ds(0 if upward else room // 2, room // 2)
        i = 0 if upward else 1
        return remote(mid_packed.at[some], got_packed.at[some], pack_fwd.at[i], pack_recv.at[i],
                      giver(up4 if upward else down4))

    def high_copy(r):
        return remote(strips.at[r], strip_of(t_cross, ring // per, lax.rem(ring, per)),
                      high_send, high_recv, at_device(r, z, hi))

    def pack_halves():
        return [(u, pl.ds(0 if u else room // 2, room // 2), 0 if u else 1) for u in (True, False)]

    def spread_start(r, carry):
        @pl.when(r == ring)
        def _():
            pltpu.make_async_copy(strip_of(t_ref.at[:, 0], r // per, lax.rem(r, per)), spread.at[ring],
                                  spread_recv).start()
            pltpu.make_async_copy(over, counts.at[ring], counts_recv).start()

        @pl.when(r != ring)
        def _():
            counts_copy(r).start()
            spread_copy(r).start()
        return carry

    def share_counts():
        arrived(counts, counts_recv)
        row_of = counts[0]
        for r in range(1, RINGS):
            row_of = jnp.where(lane == r, counts[r], row_of)
        tab_side[...] = row_of
        fetch = pltpu.make_async_copy(tab_side, counts_s, count_sem)
        fetch.start()
        fetch.wait()
        used = [jnp.maximum(counts_s[0, r] - low, 0) for r in range(RINGS)]
        ends = [used[0]]
        for r in range(1, RINGS):
            ends.append(ends[-1] + used[r])
        tile = jnp.where(lane == RINGS, ends[-1], 0)
        for r in range(RINGS):
            tile = jnp.where(lane == r, ends[r] - used[r], tile)
        tab_cross[...] = tile
        other_copy().start()
        return used, ends

    def pack(used, ends):
        def pack_one(j, carry):
            r = jnp.int32(0)
            s = j
            for q in range(RINGS):
                past = ends[q] <= j
                r = r + jnp.where(past, 1, 0)
                s = s - jnp.where(past, used[q], 0)
            packed[j] = spread[jnp.minimum(r, RINGS - 1), jnp.clip(s, 0, high - 1)]
            return carry
        lax.fori_loop(0, room, pack_one, 0)

    def deal():
        def deal_one(r, carry):
            start = starts[r]
            for s in range(high):
                strips[r, s] = got_packed[jnp.minimum(start + s, room - 1)]
            return carry
        lax.fori_loop(0, RINGS, deal_one, 0)

    def take_other(ends):
        arrived(other, other_recv)
        fetch = pltpu.make_async_copy(other, other_s, count_sem)
        fetch.start()
        fetch.wait()
        for r in range(RINGS):
            starts[r] = other_s[0, r]
        most = jnp.maximum(ends[-1], other_s[0, RINGS])
        over_ref[...] = jnp.full(over_ref.shape, jnp.where(most > room, 1, 0), jnp.int32)
        over_copy().start()

    if not high:
        over_ref[...] = jnp.zeros_like(over_ref)

    @pl.when(gives)
    def _():
        greet(giver(up4))
        greet(giver(down4))
        greet(taker(up4))
        greet(taker(down4))
        greet(partner)
        if high:
            over[...] = jnp.full(over.shape, count_ref[0, 0], jnp.int32)
            greet(giver(across))
            for d in range(1, RINGS):
                greet(at_device(lax.rem(ring + d, RINGS), z, core))
        pl.semaphore_wait(barrier, 3 + (RINGS if high else 0))
        give_copy().start()
        def launch(k):
            for upward in (True, False):
                if k:
                    cross_copy(k - 1, upward).wait_send()
                cross_copy(k, upward).start()

        def forward(k):
            for upward in (True, False):
                p = k if upward else quarter + k
                arrived(mid.at[p], mid_recv.at[p])
                fwd_copy(k, upward).start()

        launch(0)
        if high:
            lax.fori_loop(0, RINGS, spread_start, 0)
        launch(1)
        pl.semaphore_wait(ready, 2)
        forward(0)
        if high:
            used, ends = share_counts()
            arrived(spread, spread_recv)
            pack(used, ends)
            for upward in (True, False):
                pack_copy(upward).start()
        launch(2)
        forward(1)
        if high:
            take_other(ends)
            for upward, some, i in pack_halves():
                arrived(mid_packed.at[some], pack_mid.at[i])
                pack_fwd_copy(upward).start()
        launch(3)
        forward(2)
        if high:
            for upward, some, i in pack_halves():
                arrived(got_packed.at[some], pack_recv.at[i])
            deal()

            def high_start(r, carry):
                high_copy(r).start()
                return carry
            lax.fori_loop(0, RINGS, high_start, 0)
        forward(3)
        if high:
            for upward in (True, False):
                pack_copy(upward).wait_send()
                pack_fwd_copy(upward).wait_send()
            other_copy().wait_send()
            over_copy().wait_send()
            arrived(spread.at[pl.ds(0, RINGS - 1)], spread_send)
            arrived(counts.at[pl.ds(0, RINGS - 1)], counts_send)
            arrived(strips, high_send)
        give_copy().wait_send()
        for k in range(quarter):
            for upward in (True, False):
                if k == quarter - 1:
                    cross_copy(k, upward).wait_send()
                fwd_copy(k, upward).wait_send()
        got = parts.at[0, :, pl.ds(0, rows)]
        arrived(got, total_recv)
        diag_ref[0] = got[0]
        next_ref[0] = got[1]

    def side_copy():
        return remote(t_ref.at[:, 0], t_side, side_send, side_recv, side_dest)

    def tab_copy(i):
        return remote(tab, (tab_side, tab_cross)[i], tab_send.at[i], tab_recv.at[i],
                      (side_dest, taker(across))[i])

    def own_copy():
        return pltpu.make_async_copy(t_ref.at[:, 0], t_own, own_sem)

    def beside_copy():
        part = c_all.at[y, x, hi, zlo]
        return remote(part, part, beside_send, beside_recv, taker(beside))

    def unit(j):
        u = lax.rem(z // 2 + NZ // 2 + j, NZ // 2)
        return u // (HALF // 2), 2 * lax.rem(u, HALF // 2)

    def c1_copy(j, to):
        h, q = unit(j)
        part = c_all.at[y, x, h, pl.ds(q, 2)]
        dest = {1: up2, 2: up4, -1: down2, -2: down4}[j - to]
        return remote(part, part, c1_send.at[to + 4], c1_recv.at[to + 4], taker(dest))

    def c1_wait(j):
        arrived(c_all.at[y, x, 0, pl.ds(0, 2)], c1_recv.at[j + 4])

    arrivals = [[0], [-1, 1], [-2, 2], [-3, 3], [-4]]
    onwards = {0: (-1, 1, -2, 2), -1: (-3,), 1: (3,), -2: (-4,)}

    def path_of(j):
        return 1 if j >= 0 else 0

    def plane_part(j, stage, i):
        path = path_of(j)
        h, q = unit(j)
        both = pl.ds(q, 2)
        along_x = path == stage
        o = lax.rem((x if along_x else y) + (3 if i == 2 else 1), NX)
        if stage == 0:
            if i < 2:
                return c_all.at[y, x, h, both]
            return c_all.at[y if along_x else o, o if along_x else x, h, pl.ds(q + i - 2, 1)]
        if i < 2:
            return c_all.at[pl.ds(0, NY), x, h, both] if along_x else c_all.at[y, pl.ds(0, NX), h, both]
        two = pl.ds(2 * (i - 2), 2)
        return c_all.at[two, o, h, both] if along_x else c_all.at[o, two, h, both]

    def plane_copy(j, stage, i):
        part = plane_part(j, stage, i)
        dev = ([east, west] if path_of(j) == stage else [north, south])[i % 2]
        return remote(part, part, plane_send.at[j + 4, stage, i], plane_recv.at[j + 4, stage, i], dev)

    def plane_wait(j, stage, i):
        arrived(plane_part(j, stage, i), plane_recv.at[j + 4, stage, i])

    def plane_step(j, phase):
        for i in range(2):
            if phase > 0:
                plane_wait(j, (phase - 1) // 2, i + 2 * ((phase - 1) % 2))
                if phase % 2:
                    plane_copy(j, phase // 2, i + 2).start()
        if phase < 4 and phase % 2 == 0:
            for i in range(2):
                plane_copy(j, phase // 2, i).start()

    def choose(pair_of, count):
        for s in range(slots):
            pair = pair_of(s)
            live = s < count
            block = c_all[jnp.where(live, pair // (2 * NX), NY),
                          jnp.where(live, lax.rem(pair // 2, NX), 0),
                          jnp.where(live, lax.rem(pair, 2), 0)]
            for q in range(HALF):
                csel[s * bs:(s + 1) * bs, q * bs:(q + 1) * bs] = block[q]

    def half(t_buf, k):
        lhs = jnp.concatenate(
            [jnp.concatenate([t_buf[p, s] for s in range(slots)], axis=1) for p in (k, quarter + k)], axis=0)
        both = jnp.dot(lhs, csel[...], preferred_element_type=F32).astype(BF16)
        return both[:bs], both[bs:]

    ring_c = jnp.where(hi == 0, ring, lax.rem(ring + RINGS - 1, RINGS))

    def part_a(i):
        return remote(stage_a.at[i], parts.at[g], part_send.at[0], part_recv,
                      {"grp": 2 * i, "blk": 2 * ring})

    def part_b(i):
        return remote(stage_b.at[i], parts.at[g, 0], part_send.at[1], part_recv,
                      {"grp": 2 * i + 1, "blk": 2 * ring + 1})

    def part_c(i):
        return remote(stage_c.at[i], parts.at[g, 1], part_send.at[2], part_recv,
                      {"grp": 2 * i + 1, "blk": 2 * ring_c + 1})

    @pl.when(takes)
    def _():
        for dev in [partner, taker(beside), taker(up2), taker(down2), taker(up4), taker(down4), taker(across), east, west, north, south, side_source]:
            greet(dev)
        own_copy().start()
        piece_at(core)[...] = ct_ref[...]
        pl.semaphore_wait(barrier, 14)
        for dev in (giver(up4), giver(down4)):
            pl.semaphore_signal(ready, inc=1, device_id=dev, device_id_type=MESH)
        tab_copy(0).start()
        tab_copy(1).start()
        side_copy().start()
        c_all[NY, 0, 0] = jnp.zeros(c_all.shape[3:], BF16)
        gram[...] = jnp.zeros_like(gram)
        side[...] = jnp.zeros_like(side)
        arrived(piece_at(1 - core), give_recv)
        c_all[y, x, hi, zlo] = joint[...].astype(F32).T.astype(BF16)
        beside_copy().start()
        arrived(c_all.at[y, x, hi, zlo], beside_recv)
        for tick in range(len(arrivals) + 4):
            if tick < len(arrivals):
                for j in arrivals[tick]:
                    if j:
                        c1_wait(j)
                    for to in onwards.get(j, ()):
                        c1_copy(j, to).start()
            for phase in range(5):
                if 0 <= tick - phase < len(arrivals):
                    for j in arrivals[tick - phase]:
                        plane_step(j, phase)
        arrived(tab_side, tab_recv.at[0])
        arrived(tab_cross, tab_recv.at[1])
        fetch = [pltpu.make_async_copy(v, tabs.at[i], smem_sem.at[i])
                 for i, v in enumerate((tab_side, tab_cross))]
        for f in fetch:
            f.start()
        for f in fetch:
            f.wait()
        own_copy().wait()
        arrived(t_side, side_recv)

        choose(lambda s: pairs_ref[0, s], count_ref[0, 0])

        def own_step(k, carry):
            h_own[k], h_own[quarter + k] = half(t_own, k)
            return carry
        lax.fori_loop(0, quarter, own_step, 0)
        choose(lambda s: tabs[0, 0, s], tabs[0, 0, slots])

        def side_step(k, carry):
            h_side[k], h_side[quarter + k] = half(t_side, k)
            return carry
        lax.fori_loop(0, quarter, side_step, 0)
        choose(lambda s: tabs[1, 0, s], tabs[1, 0, slots])

        if high:
            arrived(t_cross.at[:, pl.ds(low, high)], high_recv)

        def cross_step(k, carry):
            for p in (k, quarter + k):
                arrived(t_cross.at[p, pl.ds(0, low)], cross_recv.at[p])
            for p, h_cross in zip((k, quarter + k), half(t_cross, k)):
                both = jnp.concatenate([h_own[p], h_cross], axis=0)
                gram[...] += nt(both, both)
                side[...] += nt(h_cross, h_side[p])
            return carry
        lax.fori_loop(0, quarter, cross_step, 0)

        def cut(block):
            return block.reshape(stage_b.shape)

        @pl.when(hi == 0)
        def _():
            stage_a[:, 0] = cut(gram[:bs, :bs])
            stage_a[:, 1] = cut(gram[:bs, bs:])
            stage_b[...] = cut(gram[bs:, bs:])
            stage_c[...] = cut(side[...])

        @pl.when(hi == 1)
        def _():
            stage_a[:, 0] = cut(gram[bs:, bs:])
            stage_a[:, 1] = cut(gram[bs:, :bs])
            stage_b[...] = cut(gram[:bs, :bs])
            stage_c[...] = cut(side[...].T)

        for i in range(HALF):
            away_a = jnp.logical_or(zlo != i, hi == 1)
            away_b = jnp.logical_or(zlo != i, hi == 0)

            @pl.when(away_a)
            def _():
                part_a(i).start()

            @pl.when(jnp.logical_not(away_a))
            def _():
                pltpu.make_async_copy(stage_a.at[i], parts.at[g], part_recv).start()

            @pl.when(away_b)
            def _():
                part_b(i).start()

            @pl.when(jnp.logical_not(away_b))
            def _():
                pltpu.make_async_copy(stage_b.at[i], parts.at[g, 0], part_recv).start()
            part_c(i).start()

        arrived(parts, part_recv)
        total[...] = jnp.sum(parts[...], axis=0) * factor
        total_copy().start()
        if high:
            arrived(over, over_recv)
            over_ref[...] = over[...]
        mine = total[:, pl.ds(pl.multiple_of(hi * rows, rows), rows)]
        diag_ref[0] = mine[0]
        next_ref[0] = mine[1]

        total_copy().wait_send()
        tab_copy(0).wait_send()
        tab_copy(1).wait_send()
        side_copy().wait_send()
        beside_copy().wait_send()
        for j, tos in onwards.items():
            for to in tos:
                c1_copy(j, to).wait_send()
        for units in arrivals:
            for j in units:
                for stage in range(2):
                    for i in range(4):
                        plane_copy(j, stage, i).wait_send()

        @pl.when(hi == 0)
        def _():
            arrived(parts.at[pl.ds(0, HALF - 1)], part_send.at[0])
            arrived(parts.at[pl.ds(0, HALF // 2)], part_send.at[1])

        @pl.when(hi == 1)
        def _():
            arrived(parts.at[pl.ds(0, HALF)], part_send.at[0])
            arrived(parts.at[pl.ds(0, HALF - 1), 0], part_send.at[1])
        arrived(parts.at[pl.ds(0, HALF // 2)], part_send.at[2])


def run(low, room, collective_id, three_centre, occupied_coefficients, paired_blocks, stored_counts):
    naux, _, slots, bs, _ = three_centre.shape
    groups = HALF * CORES
    cols = occupied_coefficients.shape[1]
    nocc = cols * groups
    factor = 1.0 / math.sqrt(naux * groups * nocc)
    rows = bs // groups
    dma = pltpu.SemaphoreType.DMA
    vmem = pl.BlockSpec(memory_space=pltpu.VMEM)
    smem = pl.BlockSpec(memory_space=pltpu.SMEM)
    slab = (naux, slots, bs, bs)
    strip = bs * naux // RINGS
    high, room = max(slots - low, 1), max(room, 1)
    tile = jax.ShapeDtypeStruct((1, 128), jnp.int32)
    return pl.pallas_call(
        functools.partial(kernel, factor, low, room),
        out_shape=[jax.ShapeDtypeStruct((1, rows, bs), F32)] * 2 + [tile],
        in_specs=[smem, smem, vmem, pl.BlockSpec(memory_space=pl.ANY)],
        out_specs=[vmem, vmem, vmem],
        scratch_shapes=[
            pltpu.VMEM((RINGS, high, strip, bs), BF16),
            pltpu.VMEM((room, strip, bs), BF16),
            pltpu.VMEM((room, strip, bs), BF16),
            pltpu.VMEM((room, strip, bs), BF16),
            pltpu.VMEM((RINGS, high, strip, bs), BF16),
            pltpu.VMEM((RINGS, 1, 128), jnp.int32),
            pltpu.VMEM((1, 128), jnp.int32),
            pltpu.VMEM((1, 128), jnp.int32),
            pltpu.SMEM((1, 128), jnp.int32),
            pltpu.SMEM((1, 128), jnp.int32),
            pltpu.SMEM((RINGS,), jnp.int32),
            dma, dma, dma, dma, dma, dma, dma, dma,
            dma((2,)), dma((2,)), dma((2,)), dma((2,)), dma, dma, dma,
            pltpu.VMEM((2 * cols, bs), BF16),
            pltpu.VMEM((NY + 1, NX, 2, HALF, bs, bs), BF16),
            pltpu.VMEM(slab, BF16),
            pltpu.VMEM(slab, BF16),
            pltpu.VMEM(slab, BF16),
            pltpu.VMEM((naux, low, bs, bs), BF16),
            pltpu.VMEM((slots * bs, nocc), BF16),
            pltpu.VMEM((naux, bs, nocc), BF16),
            pltpu.VMEM((naux, bs, nocc), BF16),
            pltpu.VMEM((2 * bs, 2 * bs), F32),
            pltpu.VMEM((bs, bs), F32),
            pltpu.VMEM((HALF, 2, 2 * rows, bs), F32),
            pltpu.VMEM((HALF, 2 * rows, bs), F32),
            pltpu.VMEM((HALF, 2 * rows, bs), F32),
            pltpu.VMEM((groups, 2, 2 * rows, bs), F32),
            pltpu.VMEM((2, 2 * rows, bs), F32),
            pltpu.VMEM((1, 128), jnp.int32),
            pltpu.VMEM((1, 128), jnp.int32),
            pltpu.VMEM((1, 128), jnp.int32),
            pltpu.SMEM((2, 1, 128), jnp.int32),
            dma, dma, dma, dma, dma((NZ // 2,)), dma((NZ // 2,)), dma((NZ // 2, 2, 4)), dma((NZ // 2, 2, 4)),
            dma((naux,)), dma((naux,)), dma((naux,)), dma((naux,)), dma, dma,
            dma((2,)), dma((2,)), dma, dma((2,)), dma((3,)), dma, dma, dma,
            pltpu.SemaphoreType.REGULAR,
        ],
        compiler_params=pltpu.CompilerParams(
            collective_id=collective_id, has_side_effects=True, vmem_limit_bytes=60 * 1024 * 1024),
        cost_estimate=pl.CostEstimate(flops=8 * 10**9, bytes_accessed=6 * 2**20, transcendentals=0),
    )(paired_blocks, stored_counts[None], occupied_coefficients.T, three_centre)


def body(*args):
    slots = args[0].shape[2]
    diag, following, over = run(STILL, ROOM, 0, *args)
    return lax.cond(over[0, 0] > 0, lambda: tuple(run(slots, 0, 1, *args)[:2]), lambda: (diag, following))


def solution(mesh):
    placed = (P("grp", "blk", None, None, None), P("blk", "grp"), P("blk", None), P("blk"))
    return jax.shard_map(
        body,
        mesh=mesh,
        in_specs=placed,
        out_specs=(P("blk", "grp", None), P("blk", "grp", None)),
        check_vma=False,
    )
```

```python
import functools
import math

import jax
import jax.numpy as jnp
from jax import lax
from jax.experimental import pallas as pl
from jax.experimental.pallas import tpu as pltpu
from jax.sharding import PartitionSpec as P

MESH = pl.DeviceIdType.MESH
F32 = jnp.float32
BF16 = jnp.bfloat16
NX, NY, NZ, HALF, CORES = 4, 4, 16, 8, 2
RINGS = NX * NY
STILL, ROOM = 4, 20


def nt(a, b):
    return lax.dot_general(a, b, (((1,), (1,)), ((), ())), preferred_element_type=F32)


def at_device(ring, z, core):
    return {
        "grp": lax.rem(z, HALF) * CORES + core,
        "blk": ring * 2 + z // HALF,
    }


def kernel(factor, low, room, pairs_ref, count_ref, ct_ref, t_ref, diag_ref, next_ref, over_ref,
           spread, packed, mid_packed, got_packed, strips, counts, other, over, counts_s, other_s, starts,
           spread_send, spread_recv, counts_send, counts_recv, other_send, other_recv, over_send, over_recv,
           pack_send, pack_mid, pack_fwd, pack_recv, high_send, high_recv, count_sem,
           joint, c_all, t_own, t_cross, t_side, mid, csel, h_own, h_side, gram, side,
           stage_a, stage_b, stage_c, parts, total, tab, tab_cross, tab_side, tabs,
           beside_send, beside_recv, give_send, give_recv, c1_send, c1_recv, plane_send, plane_recv,
           cross_send, mid_recv, fwd_send, cross_recv, side_send, side_recv,
           tab_send, tab_recv, own_sem, smem_sem, part_send, part_recv, total_send, total_recv, ready):
    naux, slots, bs = t_ref.shape[0], t_ref.shape[2], t_ref.shape[3]
    cols = ct_ref.shape[0]
    quarter = naux // 2
    high = slots - low
    per = RINGS // naux
    strip = bs // per

    g = lax.axis_index("grp")
    b = lax.axis_index("blk")
    zlo, core = g // CORES, lax.rem(g, CORES)
    ring, hi = b // 2, lax.rem(b, 2)
    y, x = ring // NX, lax.rem(ring, NX)
    z = hi * HALF + zlo
    takes = core == hi
    gives = core != hi

    def remote(src, dst, ssem, rsem, dev):
        return pltpu.make_async_remote_copy(
            src_ref=src, dst_ref=dst, send_sem=ssem, recv_sem=rsem,
            device_id=dev, device_id_type=MESH)

    def arrived(ref, sem):
        pltpu.make_async_copy(ref, ref, sem).wait()

    def ring_at(xx, yy):
        return lax.rem(yy, NY) * NX + lax.rem(xx, NX)

    def taker(zz):
        return at_device(ring, zz, zz // HALF)

    def giver(zz):
        return at_device(ring, zz, 1 - zz // HALF)

    up4, down4 = lax.rem(z + 4, NZ), lax.rem(z + NZ - 4, NZ)
    beside = z + 1 - 2 * lax.rem(z, 2)
    up2, down2 = lax.rem(z + 2, NZ), lax.rem(z + NZ - 2, NZ)
    across = lax.rem(z + HALF, NZ)
    partner = {"grp": zlo * CORES + 1 - core, "blk": b}
    step = jnp.where(hi == 0, RINGS - 1, 1)
    side_dest = at_device(lax.rem(ring + step, RINGS), z, core)
    side_source = at_device(lax.rem(ring + RINGS - step, RINGS), z, core)
    east, west = at_device(ring_at(x + 1, y), z, core), at_device(ring_at(x + 3, y), z, core)
    north, south = at_device(ring_at(x, y + 1), z, core), at_device(ring_at(x, y + 3), z, core)

    barrier = pltpu.get_barrier_semaphore()

    def greet(dev):
        pl.semaphore_signal(barrier, inc=1, device_id=dev, device_id_type=MESH)

    def cross_copy(k, upward):
        p = k if upward else quarter + k
        return remote(t_ref.at[p, 0, pl.ds(0, low)], mid.at[p], cross_send.at[p], mid_recv.at[p],
                      giver(up4 if upward else down4))

    def fwd_copy(k, upward):
        p = k if upward else quarter + k
        return remote(mid.at[p], t_cross.at[p, pl.ds(0, low)], fwd_send.at[p], cross_recv.at[p],
                      taker(up4 if upward else down4))

    rows = total.shape[1] // 2

    def total_copy():
        return remote(total.at[:, pl.ds(pl.multiple_of((1 - hi) * rows, rows), rows)],
                      parts.at[0, :, pl.ds(0, rows)], total_send, total_recv, partner)

    def piece_at(cc):
        return joint.at[pl.ds(pl.multiple_of(cc * cols, cols), cols)]

    def give_copy():
        return remote(ct_ref, piece_at(core), give_send, give_recv, partner)

    lane = lax.broadcasted_iota(jnp.int32, tab.shape, 1)
    table = jnp.where(lane == slots, count_ref[0, 0], 0)
    for s in range(slots):
        table = jnp.where(lane == s, pairs_ref[0, s], table)
    tab[...] = table

    def strip_of(t, p, part):
        return t.at[p, pl.ds(low, high), pl.ds(pl.multiple_of(part * strip, strip), strip)]

    def spread_copy(r):
        return remote(strip_of(t_ref.at[:, 0], r // per, lax.rem(r, per)), spread.at[ring],
                      spread_send, spread_recv, at_device(r, z, core))

    def counts_copy(r):
        return remote(over, counts.at[ring], counts_send, counts_recv, at_device(r, z, core))

    def other_copy():
        return remote(tab_cross, other, other_send, other_recv, giver(across))

    def over_copy():
        return remote(over_ref, over, over_send, over_recv, partner)

    def pack_copy(upward):
        some = pl.ds(0 if upward else room // 2, room // 2)
        i = 0 if upward else 1
        return remote(packed.at[some], mid_packed.at[some], pack_send.at[i], pack_mid.at[i],
                      giver(up4 if upward else down4))

    def pack_fwd_copy(upward):
        some = pl.ds(0 if upward else room // 2, room // 2)
        i = 0 if upward else 1
        return remote(mid_packed.at[some], got_packed.at[some], pack_fwd.at[i], pack_recv.at[i],
                      giver(up4 if upward else down4))

    def high_copy(r):
        return remote(strips.at[r], strip_of(t_cross, ring // per, lax.rem(ring, per)),
                      high_send, high_recv, at_device(r, z, hi))

    def pack_halves():
        return [(u, pl.ds(0 if u else room // 2, room // 2), 0 if u else 1) for u in (True, False)]

    def spread_start(r, carry):
        @pl.when(r == ring)
        def _():
            pltpu.make_async_copy(strip_of(t_ref.at[:, 0], r // per, lax.rem(r, per)), spread.at[ring],
                                  spread_recv).start()
            pltpu.make_async_copy(over, counts.at[ring], counts_recv).start()

        @pl.when(r != ring)
        def _():
            counts_copy(r).start()
            spread_copy(r).start()
        return carry

    def share_counts():
        arrived(counts, counts_recv)
        row_of = counts[0]
        for r in range(1, RINGS):
            row_of = jnp.where(lane == r, counts[r], row_of)
        tab_side[...] = row_of
        fetch = pltpu.make_async_copy(tab_side, counts_s, count_sem)
        fetch.start()
        fetch.wait()
        used = [jnp.maximum(counts_s[0, r] - low, 0) for r in range(RINGS)]
        ends = [used[0]]
        for r in range(1, RINGS):
            ends.append(ends[-1] + used[r])
        tile = jnp.where(lane == RINGS, ends[-1], 0)
        for r in range(RINGS):
            tile = jnp.where(lane == r, ends[r] - used[r], tile)
        tab_cross[...] = tile
        other_copy().start()
        return used, ends

    def pack(used, ends):
        def pack_one(j, carry):
            r = jnp.int32(0)
            s = j
            for q in range(RINGS):
                past = ends[q] <= j
                r = r + jnp.where(past, 1, 0)
                s = s - jnp.where(past, used[q], 0)
            packed[j] = spread[jnp.minimum(r, RINGS - 1), jnp.clip(s, 0, high - 1)]
            return carry
        lax.fori_loop(0, room, pack_one, 0)

    def deal():
        def deal_one(r, carry):
            start = starts[r]
            for s in range(high):
                strips[r, s] = got_packed[jnp.minimum(start + s, room - 1)]
            return carry
        lax.fori_loop(0, RINGS, deal_one, 0)

    def take_other(ends):
        arrived(other, other_recv)
        fetch = pltpu.make_async_copy(other, other_s, count_sem)
        fetch.start()
        fetch.wait()
        for r in range(RINGS):
            starts[r] = other_s[0, r]
        most = jnp.maximum(ends[-1], other_s[0, RINGS])
        over_ref[...] = jnp.full(over_ref.shape, jnp.where(most > room, 1, 0), jnp.int32)
        over_copy().start()

    if not high:
        over_ref[...] = jnp.zeros_like(over_ref)

    @pl.when(gives)
    def _():
        greet(giver(up4))
        greet(giver(down4))
        greet(taker(up4))
        greet(taker(down4))
        greet(partner)
        if high:
            over[...] = jnp.full(over.shape, count_ref[0, 0], jnp.int32)
            greet(giver(across))
            for d in range(1, RINGS):
                greet(at_device(lax.rem(ring + d, RINGS), z, core))
        pl.semaphore_wait(barrier, 3 + (RINGS if high else 0))
        give_copy().start()
        def launch(k):
            for upward in (True, False):
                if k:
                    cross_copy(k - 1, upward).wait_send()
                cross_copy(k, upward).start()

        def forward(k):
            for upward in (True, False):
                p = k if upward else quarter + k
                arrived(mid.at[p], mid_recv.at[p])
                fwd_copy(k, upward).start()

        if high:
            lax.fori_loop(0, RINGS, spread_start, 0)
        launch(0)
        launch(1)
        pl.semaphore_wait(ready, 2)
        forward(0)
        launch(2)
        if high:
            used, ends = share_counts()
            arrived(spread, spread_recv)
            pack(used, ends)
            for upward in (True, False):
                pack_copy(upward).start()
        forward(1)
        if high:
            for upward, some, i in pack_halves():
                arrived(mid_packed.at[some], pack_mid.at[i])
                pack_fwd_copy(upward).start()
        launch(3)
        forward(2)
        if high:
            for upward, some, i in pack_halves():
                arrived(got_packed.at[some], pack_recv.at[i])
            take_other(ends)
            deal()

            def high_start(r, carry):
                high_copy(r).start()
                return carry
            lax.fori_loop(0, RINGS, high_start, 0)
        forward(3)
        if high:
            for upward in (True, False):
                pack_copy(upward).wait_send()
                pack_fwd_copy(upward).wait_send()
            other_copy().wait_send()
            over_copy().wait_send()
            arrived(spread.at[pl.ds(0, RINGS - 1)], spread_send)
            arrived(counts.at[pl.ds(0, RINGS - 1)], counts_send)
            arrived(strips, high_send)
        give_copy().wait_send()
        for k in range(quarter):
            for upward in (True, False):
                if k == quarter - 1:
                    cross_copy(k, upward).wait_send()
                fwd_copy(k, upward).wait_send()
        got = parts.at[0, :, pl.ds(0, rows)]
        arrived(got, total_recv)
        diag_ref[0] = got[0]
        next_ref[0] = got[1]

    def side_copy():
        return remote(t_ref.at[:, 0], t_side, side_send, side_recv, side_dest)

    def tab_copy(i):
        return remote(tab, (tab_side, tab_cross)[i], tab_send.at[i], tab_recv.at[i],
                      (side_dest, taker(across))[i])

    def own_copy():
        return pltpu.make_async_copy(t_ref.at[:, 0], t_own, own_sem)

    def beside_copy():
        part = c_all.at[y, x, hi, zlo]
        return remote(part, part, beside_send, beside_recv, taker(beside))

    def unit(j):
        u = lax.rem(z // 2 + NZ // 2 + j, NZ // 2)
        return u // (HALF // 2), 2 * lax.rem(u, HALF // 2)

    def c1_copy(j, to):
        h, q = unit(j)
        part = c_all.at[y, x, h, pl.ds(q, 2)]
        dest = {1: up2, 2: up4, -1: down2, -2: down4}[j - to]
        return remote(part, part, c1_send.at[to + 4], c1_recv.at[to + 4], taker(dest))

    def c1_wait(j):
        arrived(c_all.at[y, x, 0, pl.ds(0, 2)], c1_recv.at[j + 4])

    arrivals = [[0], [-1, 1], [-2, 2], [-3, 3], [-4]]
    onwards = {0: (-1, 1, -2, 2), -1: (-3,), 1: (3,), -2: (-4,)}

    def path_of(j):
        return 1 if j >= 0 else 0

    def plane_part(j, stage, i):
        path = path_of(j)
        h, q = unit(j)
        both = pl.ds(q, 2)
        along_x = path == stage
        o = lax.rem((x if along_x else y) + (3 if i == 2 else 1), NX)
        if stage == 0:
            if i < 2:
                return c_all.at[y, x, h, both]
            return c_all.at[y if along_x else o, o if along_x else x, h, pl.ds(q + i - 2, 1)]
        if i < 2:
            return c_all.at[pl.ds(0, NY), x, h, both] if along_x else c_all.at[y, pl.ds(0, NX), h, both]
        two = pl.ds(2 * (i - 2), 2)
        return c_all.at[two, o, h, both] if along_x else c_all.at[o, two, h, both]

    def plane_copy(j, stage, i):
        part = plane_part(j, stage, i)
        dev = ([east, west] if path_of(j) == stage else [north, south])[i % 2]
        return remote(part, part, plane_send.at[j + 4], plane_recv.at[j + 4, stage, i], dev)

    def plane_wait(j, stage, i):
        arrived(plane_part(j, stage, i), plane_recv.at[j + 4, stage, i])

    def plane_step(j, phase):
        for i in range(2):
            if phase > 0:
                plane_wait(j, (phase - 1) // 2, i + 2 * ((phase - 1) % 2))
                if phase % 2:
                    plane_copy(j, phase // 2, i + 2).start()
        if phase < 4 and phase % 2 == 0:
            for i in range(2):
                plane_copy(j, phase // 2, i).start()

    def choose(pair_of, count):
        for s in range(slots):
            pair = pair_of(s)
            live = s < count
            block = c_all[jnp.where(live, pair // (2 * NX), NY),
                          jnp.where(live, lax.rem(pair // 2, NX), 0),
                          jnp.where(live, lax.rem(pair, 2), 0)]
            for q in range(HALF):
                csel[s * bs:(s + 1) * bs, q * bs:(q + 1) * bs] = block[q]

    def half(t_buf, k):
        lhs = jnp.concatenate(
            [jnp.concatenate([t_buf[p, s] for s in range(slots)], axis=1) for p in (k, quarter + k)], axis=0)
        both = jnp.dot(lhs, csel[...], preferred_element_type=F32).astype(BF16)
        return both[:bs], both[bs:]

    ring_c = jnp.where(hi == 0, ring, lax.rem(ring + RINGS - 1, RINGS))

    def part_a(i):
        return remote(stage_a.at[i], parts.at[g], part_send.at[0], part_recv,
                      {"grp": 2 * i, "blk": 2 * ring})

    def part_b(i):
        return remote(stage_b.at[i], parts.at[g, 0], part_send.at[1], part_recv,
                      {"grp": 2 * i + 1, "blk": 2 * ring + 1})

    def part_c(i):
        return remote(stage_c.at[i], parts.at[g, 1], part_send.at[2], part_recv,
                      {"grp": 2 * i + 1, "blk": 2 * ring_c + 1})

    @pl.when(takes)
    def _():
        for dev in [partner, taker(beside), taker(up2), taker(down2), taker(up4), taker(down4), taker(across), east, west, north, south, side_source]:
            greet(dev)
        own_copy().start()
        piece_at(core)[...] = ct_ref[...]
        pl.semaphore_wait(barrier, 14)
        for dev in (giver(up4), giver(down4)):
            pl.semaphore_signal(ready, inc=1, device_id=dev, device_id_type=MESH)
        tab_copy(0).start()
        tab_copy(1).start()
        side_copy().start()
        c_all[NY, 0, 0] = jnp.zeros(c_all.shape[3:], BF16)
        gram[...] = jnp.zeros_like(gram)
        side[...] = jnp.zeros_like(side)
        arrived(piece_at(1 - core), give_recv)
        c_all[y, x, hi, zlo] = joint[...].astype(F32).T.astype(BF16)
        beside_copy().start()
        arrived(c_all.at[y, x, hi, zlo], beside_recv)
        for tick in range(len(arrivals) + 4):
            if tick < len(arrivals):
                for j in arrivals[tick]:
                    if j:
                        c1_wait(j)
                    for to in onwards.get(j, ()):
                        c1_copy(j, to).start()
            for phase in range(5):
                if 0 <= tick - phase < len(arrivals):
                    for j in arrivals[tick - phase]:
                        plane_step(j, phase)
        arrived(tab_side, tab_recv.at[0])
        arrived(tab_cross, tab_recv.at[1])
        fetch = [pltpu.make_async_copy(v, tabs.at[i], smem_sem.at[i])
                 for i, v in enumerate((tab_side, tab_cross))]
        for f in fetch:
            f.start()
        for f in fetch:
            f.wait()
        own_copy().wait()
        arrived(t_side, side_recv)

        choose(lambda s: pairs_ref[0, s], count_ref[0, 0])

        def own_step(k, carry):
            h_own[k], h_own[quarter + k] = half(t_own, k)
            return carry
        lax.fori_loop(0, quarter, own_step, 0)
        choose(lambda s: tabs[0, 0, s], tabs[0, 0, slots])

        def side_step(k, carry):
            h_side[k], h_side[quarter + k] = half(t_side, k)
            return carry
        lax.fori_loop(0, quarter, side_step, 0)
        choose(lambda s: tabs[1, 0, s], tabs[1, 0, slots])

        if high:
            arrived(t_cross.at[:, pl.ds(low, high)], high_recv)

        def cross_step(k, carry):
            for p in (k, quarter + k):
                arrived(t_cross.at[p, pl.ds(0, low)], cross_recv.at[p])
            for p, h_cross in zip((k, quarter + k), half(t_cross, k)):
                both = jnp.concatenate([h_own[p], h_cross], axis=0)
                gram[...] += nt(both, both)
                side[...] += nt(h_cross, h_side[p])
            return carry
        lax.fori_loop(0, quarter, cross_step, 0)

        def cut(block):
            return block.reshape(stage_b.shape)

        @pl.when(hi == 0)
        def _():
            stage_a[:, 0] = cut(gram[:bs, :bs])
            stage_a[:, 1] = cut(gram[:bs, bs:])
            stage_b[...] = cut(gram[bs:, bs:])
            stage_c[...] = cut(side[...])

        @pl.when(hi == 1)
        def _():
            stage_a[:, 0] = cut(gram[bs:, bs:])
            stage_a[:, 1] = cut(gram[bs:, :bs])
            stage_b[...] = cut(gram[:bs, :bs])
            stage_c[...] = cut(side[...].T)

        for i in range(HALF):
            away_a = jnp.logical_or(zlo != i, hi == 1)
            away_b = jnp.logical_or(zlo != i, hi == 0)

            @pl.when(away_a)
            def _():
                part_a(i).start()

            @pl.when(jnp.logical_not(away_a))
            def _():
                pltpu.make_async_copy(stage_a.at[i], parts.at[g], part_recv).start()

            @pl.when(away_b)
            def _():
                part_b(i).start()

            @pl.when(jnp.logical_not(away_b))
            def _():
                pltpu.make_async_copy(stage_b.at[i], parts.at[g, 0], part_recv).start()
            part_c(i).start()

        arrived(parts, part_recv)
        total[...] = jnp.sum(parts[...], axis=0) * factor
        total_copy().start()
        if high:
            arrived(over, over_recv)
            over_ref[...] = over[...]
        mine = total[:, pl.ds(pl.multiple_of(hi * rows, rows), rows)]
        diag_ref[0] = mine[0]
        next_ref[0] = mine[1]

        total_copy().wait_send()
        tab_copy(0).wait_send()
        tab_copy(1).wait_send()
        side_copy().wait_send()
        beside_copy().wait_send()
        for j, tos in onwards.items():
            for to in tos:
                c1_copy(j, to).wait_send()
        for units in arrivals:
            for j in units:
                arrived(c_all.at[pl.ds(0, NY + 1), pl.ds(0, NX - 1), 0, pl.ds(0, 2)], plane_send.at[j + 4])

        @pl.when(hi == 0)
        def _():
            arrived(parts.at[pl.ds(0, HALF - 1)], part_send.at[0])
            arrived(parts.at[pl.ds(0, HALF // 2)], part_send.at[1])

        @pl.when(hi == 1)
        def _():
            arrived(parts.at[pl.ds(0, HALF)], part_send.at[0])
            arrived(parts.at[pl.ds(0, HALF - 1), 0], part_send.at[1])
        arrived(parts.at[pl.ds(0, HALF // 2)], part_send.at[2])


def run(low, room, collective_id, three_centre, occupied_coefficients, paired_blocks, stored_counts):
    naux, _, slots, bs, _ = three_centre.shape
    groups = HALF * CORES
    cols = occupied_coefficients.shape[1]
    nocc = cols * groups
    factor = 1.0 / math.sqrt(naux * groups * nocc)
    rows = bs // groups
    dma = pltpu.SemaphoreType.DMA
    vmem = pl.BlockSpec(memory_space=pltpu.VMEM)
    smem = pl.BlockSpec(memory_space=pltpu.SMEM)
    slab = (naux, slots, bs, bs)
    strip = bs * naux // RINGS
    high, room = max(slots - low, 1), max(room, 1)
    tile = jax.ShapeDtypeStruct((1, 128), jnp.int32)
    return pl.pallas_call(
        functools.partial(kernel, factor, low, room),
        out_shape=[jax.ShapeDtypeStruct((1, rows, bs), F32)] * 2 + [tile],
        in_specs=[smem, smem, vmem, pl.BlockSpec(memory_space=pl.ANY)],
        out_specs=[vmem, vmem, vmem],
        scratch_shapes=[
            pltpu.VMEM((RINGS, high, strip, bs), BF16),
            pltpu.VMEM((room, strip, bs), BF16),
            pltpu.VMEM((room, strip, bs), BF16),
            pltpu.VMEM((room, strip, bs), BF16),
            pltpu.VMEM((RINGS, high, strip, bs), BF16),
            pltpu.VMEM((RINGS, 1, 128), jnp.int32),
            pltpu.VMEM((1, 128), jnp.int32),
            pltpu.VMEM((1, 128), jnp.int32),
            pltpu.SMEM((1, 128), jnp.int32),
            pltpu.SMEM((1, 128), jnp.int32),
            pltpu.SMEM((RINGS,), jnp.int32),
            dma, dma, dma, dma, dma, dma, dma, dma,
            dma((2,)), dma((2,)), dma((2,)), dma((2,)), dma, dma, dma,
            pltpu.VMEM((2 * cols, bs), BF16),
            pltpu.VMEM((NY + 1, NX, 2, HALF, bs, bs), BF16),
            pltpu.VMEM(slab, BF16),
            pltpu.VMEM(slab, BF16),
            pltpu.VMEM(slab, BF16),
            pltpu.VMEM((naux, low, bs, bs), BF16),
            pltpu.VMEM((slots * bs, nocc), BF16),
            pltpu.VMEM((naux, bs, nocc), BF16),
            pltpu.VMEM((naux, bs, nocc), BF16),
            pltpu.VMEM((2 * bs, 2 * bs), F32),
            pltpu.VMEM((bs, bs), F32),
            pltpu.VMEM((HALF, 2, 2 * rows, bs), F32),
            pltpu.VMEM((HALF, 2 * rows, bs), F32),
            pltpu.VMEM((HALF, 2 * rows, bs), F32),
            pltpu.VMEM((groups, 2, 2 * rows, bs), F32),
            pltpu.VMEM((2, 2 * rows, bs), F32),
            pltpu.VMEM((1, 128), jnp.int32),
            pltpu.VMEM((1, 128), jnp.int32),
            pltpu.VMEM((1, 128), jnp.int32),
            pltpu.SMEM((2, 1, 128), jnp.int32),
            dma, dma, dma, dma, dma((NZ // 2,)), dma((NZ // 2,)), dma((NZ // 2,)), dma((NZ // 2, 2, 4)),
            dma((naux,)), dma((naux,)), dma((naux,)), dma((naux,)), dma, dma,
            dma((2,)), dma((2,)), dma, dma((2,)), dma((3,)), dma, dma, dma,
            pltpu.SemaphoreType.REGULAR,
        ],
        compiler_params=pltpu.CompilerParams(
            collective_id=collective_id, has_side_effects=True, vmem_limit_bytes=60 * 1024 * 1024),
        cost_estimate=pl.CostEstimate(flops=8 * 10**9, bytes_accessed=6 * 2**20, transcendentals=0),
    )(paired_blocks, stored_counts[None], occupied_coefficients.T, three_centre)


def body(*args):
    slots = args[0].shape[2]
    diag, following, over = run(STILL, ROOM, 0, *args)
    return lax.cond(over[0, 0] > 0, lambda: tuple(run(slots, 0, 1, *args)[:2]), lambda: (diag, following))


def solution(mesh):
    placed = (P("grp", "blk", None, None, None), P("blk", "grp"), P("blk", None), P("blk"))
    return jax.shard_map(
        body,
        mesh=mesh,
        in_specs=placed,
        out_specs=(P("blk", "grp", None), P("blk", "grp", None)),
        check_vma=False,
    )
```

```python
import functools
import math

import jax
import jax.numpy as jnp
from jax import lax
from jax.experimental import pallas as pl
from jax.experimental.pallas import tpu as pltpu
from jax.sharding import PartitionSpec as P

MESH = pl.DeviceIdType.MESH
F32 = jnp.float32
BF16 = jnp.bfloat16
NX, NY, NZ, HALF, CORES = 4, 4, 16, 8, 2
RINGS = NX * NY
STILL, ROOM = 4, 20


def nt(a, b):
    return lax.dot_general(a, b, (((1,), (1,)), ((), ())), preferred_element_type=F32)


def at_device(ring, z, core):
    return {
        "grp": lax.rem(z, HALF) * CORES + core,
        "blk": ring * 2 + z // HALF,
    }


def kernel(factor, low, room, pairs_ref, count_ref, ct_ref, t_ref, diag_ref, next_ref, over_ref,
           spread, packed, mid_packed, got_packed, strips, counts, other, over, counts_s, other_s, starts,
           spread_send, spread_recv, counts_send, counts_recv, other_send, other_recv, over_send, over_recv,
           pack_send, pack_mid, pack_fwd, pack_recv, high_send, high_recv, count_sem,
           joint, c_all, t_own, t_cross, t_side, mid, csel, h_own, h_side, gram, side,
           stage_a, stage_b, stage_c, parts, total, tab, tab_cross, tab_side, tabs,
           beside_send, beside_recv, give_send, give_recv, c1_send, c1_recv, plane_send, plane_recv,
           cross_send, mid_recv, fwd_send, cross_recv, side_send, side_recv,
           tab_send, tab_recv, own_sem, smem_sem, part_send, part_recv, total_send, total_recv, ready):
    naux, slots, bs = t_ref.shape[0], t_ref.shape[2], t_ref.shape[3]
    cols = ct_ref.shape[0]
    quarter = naux // 2
    high = slots - low
    per = RINGS // naux
    strip = bs // per

    g = lax.axis_index("grp")
    b = lax.axis_index("blk")
    zlo, core = g // CORES, lax.rem(g, CORES)
    ring, hi = b // 2, lax.rem(b, 2)
    y, x = ring // NX, lax.rem(ring, NX)
    z = hi * HALF + zlo
    takes = core == hi
    gives = core != hi

    def remote(src, dst, ssem, rsem, dev):
        return pltpu.make_async_remote_copy(
            src_ref=src, dst_ref=dst, send_sem=ssem, recv_sem=rsem,
            device_id=dev, device_id_type=MESH)

    def arrived(ref, sem):
        pltpu.make_async_copy(ref, ref, sem).wait()

    def ring_at(xx, yy):
        return lax.rem(yy, NY) * NX + lax.rem(xx, NX)

    def taker(zz):
        return at_device(ring, zz, zz // HALF)

    def giver(zz):
        return at_device(ring, zz, 1 - zz // HALF)

    up4, down4 = lax.rem(z + 4, NZ), lax.rem(z + NZ - 4, NZ)
    beside = z + 1 - 2 * lax.rem(z, 2)
    up2, down2 = lax.rem(z + 2, NZ), lax.rem(z + NZ - 2, NZ)
    across = lax.rem(z + HALF, NZ)
    partner = {"grp": zlo * CORES + 1 - core, "blk": b}
    step = jnp.where(hi == 0, RINGS - 1, 1)
    side_dest = at_device(lax.rem(ring + step, RINGS), z, core)
    side_source = at_device(lax.rem(ring + RINGS - step, RINGS), z, core)
    east, west = at_device(ring_at(x + 1, y), z, core), at_device(ring_at(x + 3, y), z, core)
    north, south = at_device(ring_at(x, y + 1), z, core), at_device(ring_at(x, y + 3), z, core)

    barrier = pltpu.get_barrier_semaphore()

    def greet(dev):
        pl.semaphore_signal(barrier, inc=1, device_id=dev, device_id_type=MESH)

    def cross_copy(k, upward):
        p = k if upward else quarter + k
        return remote(t_ref.at[p, 0, pl.ds(0, low)], mid.at[p], cross_send.at[p], mid_recv.at[p],
                      giver(up4 if upward else down4))

    def fwd_copy(k, upward):
        p = k if upward else quarter + k
        return remote(mid.at[p], t_cross.at[p, pl.ds(0, low)], fwd_send.at[p], cross_recv.at[p],
                      taker(up4 if upward else down4))

    rows = total.shape[1] // 2

    def total_copy():
        return remote(total.at[:, pl.ds(pl.multiple_of((1 - hi) * rows, rows), rows)],
                      parts.at[0, :, pl.ds(0, rows)], total_send, total_recv, partner)

    def piece_at(cc):
        return joint.at[pl.ds(pl.multiple_of(cc * cols, cols), cols)]

    def give_copy():
        return remote(ct_ref, piece_at(core), give_send, give_recv, partner)

    lane = lax.broadcasted_iota(jnp.int32, tab.shape, 1)
    table = jnp.where(lane == slots, count_ref[0, 0], 0)
    for s in range(slots):
        table = jnp.where(lane == s, pairs_ref[0, s], table)
    tab[...] = table

    def strip_of(t, p, part):
        return t.at[p, pl.ds(low, high), pl.ds(pl.multiple_of(part * strip, strip), strip)]

    def spread_copy(r):
        return remote(strip_of(t_ref.at[:, 0], r // per, lax.rem(r, per)), spread.at[ring],
                      spread_send, spread_recv, at_device(r, z, core))

    def counts_copy(r):
        return remote(over, counts.at[ring], counts_send, counts_recv, at_device(r, z, core))

    def other_copy():
        return remote(tab_cross, other, other_send, other_recv, giver(across))

    def over_copy():
        return remote(over_ref, over, over_send, over_recv, partner)

    def pack_copy(upward):
        some = pl.ds(0 if upward else room // 2, room // 2)
        i = 0 if upward else 1
        return remote(packed.at[some], mid_packed.at[some], pack_send.at[i], pack_mid.at[i],
                      giver(up4 if upward else down4))

    def pack_fwd_copy(upward):
        some = pl.ds(0 if upward else room // 2, room // 2)
        i = 0 if upward else 1
        return remote(mid_packed.at[some], got_packed.at[some], pack_fwd.at[i], pack_recv.at[i],
                      giver(up4 if upward else down4))

    def high_copy(r):
        return remote(strips.at[r], strip_of(t_cross, ring // per, lax.rem(ring, per)),
                      high_send, high_recv, at_device(r, z, hi))

    def pack_halves():
        return [(u, pl.ds(0 if u else room // 2, room // 2), 0 if u else 1) for u in (True, False)]

    def spread_start(r, carry):
        @pl.when(r == ring)
        def _():
            pltpu.make_async_copy(strip_of(t_ref.at[:, 0], r // per, lax.rem(r, per)), spread.at[ring],
                                  spread_recv).start()
            pltpu.make_async_copy(over, counts.at[ring], counts_recv).start()

        @pl.when(r != ring)
        def _():
            counts_copy(r).start()
            spread_copy(r).start()
        return carry

    def share_counts():
        arrived(counts, counts_recv)
        row_of = counts[0]
        for r in range(1, RINGS):
            row_of = jnp.where(lane == r, counts[r], row_of)
        tab_side[...] = row_of
        fetch = pltpu.make_async_copy(tab_side, counts_s, count_sem)
        fetch.start()
        fetch.wait()
        used = [jnp.maximum(counts_s[0, r] - low, 0) for r in range(RINGS)]
        ends = [used[0]]
        for r in range(1, RINGS):
            ends.append(ends[-1] + used[r])
        tile = jnp.where(lane == RINGS, ends[-1], 0)
        for r in range(RINGS):
            tile = jnp.where(lane == r, ends[r] - used[r], tile)
        tab_cross[...] = tile
        other_copy().start()
        return used, ends

    def pack(used, ends):
        def pack_one(j, carry):
            r = jnp.int32(0)
            s = j
            for q in range(RINGS):
                past = ends[q] <= j
                r = r + jnp.where(past, 1, 0)
                s = s - jnp.where(past, used[q], 0)
            packed[j] = spread[jnp.minimum(r, RINGS - 1), jnp.clip(s, 0, high - 1)]
            return carry
        lax.fori_loop(0, room, pack_one, 0)

    def deal():
        def deal_one(r, carry):
            start = starts[r]
            for s in range(high):
                strips[r, s] = got_packed[jnp.minimum(start + s, room - 1)]
            return carry
        lax.fori_loop(0, RINGS, deal_one, 0)

    def take_other(ends):
        arrived(other, other_recv)
        fetch = pltpu.make_async_copy(other, other_s, count_sem)
        fetch.start()
        fetch.wait()
        for r in range(RINGS):
            starts[r] = other_s[0, r]
        most = jnp.maximum(ends[-1], other_s[0, RINGS])
        over_ref[...] = jnp.full(over_ref.shape, jnp.where(most > room, 1, 0), jnp.int32)
        over_copy().start()

    if not high:
        over_ref[...] = jnp.zeros_like(over_ref)

    @pl.when(gives)
    def _():
        greet(giver(up4))
        greet(giver(down4))
        greet(taker(up4))
        greet(taker(down4))
        greet(partner)
        if high:
            over[...] = jnp.full(over.shape, count_ref[0, 0], jnp.int32)
            greet(giver(across))
            for d in range(1, RINGS):
                greet(at_device(lax.rem(ring + d, RINGS), z, core))
        pl.semaphore_wait(barrier, 3 + (RINGS if high else 0))
        give_copy().start()
        def launch(k):
            for upward in (True, False):
                if k:
                    cross_copy(k - 1, upward).wait_send()
                cross_copy(k, upward).start()

        def forward(k):
            for upward in (True, False):
                p = k if upward else quarter + k
                arrived(mid.at[p], mid_recv.at[p])
                fwd_copy(k, upward).start()

        if high:
            lax.fori_loop(0, RINGS, spread_start, 0)
        launch(0)
        launch(1)
        pl.semaphore_wait(ready, 2)
        forward(0)
        launch(2)
        if high:
            used, ends = share_counts()
            arrived(spread, spread_recv)
            pack(used, ends)
            for upward in (True, False):
                pack_copy(upward).start()
        forward(1)
        if high:
            for upward, some, i in pack_halves():
                arrived(mid_packed.at[some], pack_mid.at[i])
                pack_fwd_copy(upward).start()
        launch(3)
        forward(2)
        if high:
            for upward, some, i in pack_halves():
                arrived(got_packed.at[some], pack_recv.at[i])
            take_other(ends)
            deal()

            def high_start(r, carry):
                high_copy(r).start()
                return carry
            lax.fori_loop(0, RINGS, high_start, 0)
        forward(3)
        if high:
            for upward in (True, False):
                pack_copy(upward).wait_send()
                pack_fwd_copy(upward).wait_send()
            other_copy().wait_send()
            over_copy().wait_send()
            arrived(spread.at[pl.ds(0, RINGS - 1)], spread_send)
            arrived(counts.at[pl.ds(0, RINGS - 1)], counts_send)
            arrived(strips, high_send)
        give_copy().wait_send()
        for k in range(quarter):
            for upward in (True, False):
                if k == quarter - 1:
                    cross_copy(k, upward).wait_send()
                fwd_copy(k, upward).wait_send()
        got = parts.at[0, :, pl.ds(0, rows)]
        arrived(got, total_recv)
        diag_ref[0] = got[0]
        next_ref[0] = got[1]

    def side_copy():
        return remote(t_ref.at[:, 0], t_side, side_send, side_recv, side_dest)

    def tab_copy(i):
        return remote(tab, (tab_side, tab_cross)[i], tab_send.at[i], tab_recv.at[i],
                      (side_dest, taker(across))[i])

    def own_copy():
        return pltpu.make_async_copy(t_ref.at[:, 0], t_own, own_sem)

    def beside_copy():
        part = c_all.at[y, x, hi, zlo]
        return remote(part, part, beside_send, beside_recv, taker(beside))

    def unit(j):
        u = lax.rem(z // 2 + NZ // 2 + j, NZ // 2)
        return u // (HALF // 2), 2 * lax.rem(u, HALF // 2)

    def c1_copy(j, to):
        h, q = unit(j)
        part = c_all.at[y, x, h, pl.ds(q, 2)]
        dest = {1: up2, 2: up4, -1: down2, -2: down4}[j - to]
        return remote(part, part, c1_send.at[to + 4], c1_recv.at[to + 4], taker(dest))

    def c1_wait(j):
        arrived(c_all.at[y, x, 0, pl.ds(0, 2)], c1_recv.at[j + 4])

    arrivals = [[0], [-1, 1], [-2, 2], [-3, 3], [-4]]
    onwards = {0: (-1, 1, -2, 2), -1: (-3,), 1: (3,), -2: (-4,)}

    def path_of(j):
        return 1 if j >= 0 else 0

    def plane_part(j, stage, i):
        path = path_of(j)
        h, q = unit(j)
        both = pl.ds(q, 2)
        along_x = path == stage
        o = lax.rem((x if along_x else y) + (3 if i == 2 else 1), NX)
        if stage == 0:
            if i < 2:
                return c_all.at[y, x, h, both]
            return c_all.at[y if along_x else o, o if along_x else x, h, pl.ds(q + i - 2, 1)]
        if i < 2:
            return c_all.at[pl.ds(0, NY), x, h, both] if along_x else c_all.at[y, pl.ds(0, NX), h, both]
        two = pl.ds(2 * (i - 2), 2)
        return c_all.at[two, o, h, both] if along_x else c_all.at[o, two, h, both]

    def plane_copy(j, stage, i):
        part = plane_part(j, stage, i)
        dev = ([east, west] if path_of(j) == stage else [north, south])[i % 2]
        return remote(part, part, plane_send.at[j + 4], plane_recv.at[j + 4, stage, i], dev)

    def plane_wait(j, stage, i):
        arrived(plane_part(j, stage, i), plane_recv.at[j + 4, stage, i])

    def plane_step(j, phase):
        for i in range(2):
            if phase > 0:
                plane_wait(j, (phase - 1) // 2, i + 2 * ((phase - 1) % 2))
                if phase % 2:
                    plane_copy(j, phase // 2, i + 2).start()
        if phase < 4 and phase % 2 == 0:
            for i in range(2):
                plane_copy(j, phase // 2, i).start()

    def choose(pair_of, count):
        for s in range(slots):
            pair = pair_of(s)
            live = s < count
            block = c_all[jnp.where(live, pair // (2 * NX), NY),
                          jnp.where(live, lax.rem(pair // 2, NX), 0),
                          jnp.where(live, lax.rem(pair, 2), 0)]
            for q in range(HALF):
                csel[s * bs:(s + 1) * bs, q * bs:(q + 1) * bs] = block[q]

    def half(t_buf, k):
        lhs = jnp.concatenate(
            [jnp.concatenate([t_buf[p, s] for s in range(slots)], axis=1) for p in (k, quarter + k)], axis=0)
        both = jnp.dot(lhs, csel[...], preferred_element_type=F32).astype(BF16)
        return both[:bs], both[bs:]

    ring_c = jnp.where(hi == 0, ring, lax.rem(ring + RINGS - 1, RINGS))

    def part_a(i):
        return remote(stage_a.at[i], parts.at[g], part_send.at[0], part_recv,
                      {"grp": 2 * i, "blk": 2 * ring})

    def part_b(i):
        return remote(stage_b.at[i], parts.at[g, 0], part_send.at[1], part_recv,
                      {"grp": 2 * i + 1, "blk": 2 * ring + 1})

    def part_c(i):
        return remote(stage_c.at[i], parts.at[g, 1], part_send.at[2], part_recv,
                      {"grp": 2 * i + 1, "blk": 2 * ring_c + 1})

    @pl.when(takes)
    def _():
        for dev in [partner, taker(beside), taker(up2), taker(down2), taker(up4), taker(down4), taker(across), east, west, north, south, side_source]:
            greet(dev)
        own_copy().start()
        piece_at(core)[...] = ct_ref[...]
        pl.semaphore_wait(barrier, 14)
        for dev in (giver(up4), giver(down4)):
            pl.semaphore_signal(ready, inc=1, device_id=dev, device_id_type=MESH)
        tab_copy(0).start()
        tab_copy(1).start()
        side_copy().start()
        c_all[NY, 0, 0] = jnp.zeros(c_all.shape[3:], BF16)
        gram[...] = jnp.zeros_like(gram)
        side[...] = jnp.zeros_like(side)
        arrived(piece_at(1 - core), give_recv)
        c_all[y, x, hi, zlo] = joint[...].astype(F32).T.astype(BF16)
        beside_copy().start()
        arrived(c_all.at[y, x, hi, zlo], beside_recv)
        fetch = [pltpu.make_async_copy(v, tabs.at[i], smem_sem.at[i])
                 for i, v in enumerate((tab_side, tab_cross))]
        for tick in range(len(arrivals) + 4):
            if tick == len(arrivals):
                arrived(tab_side, tab_recv.at[0])
                arrived(tab_cross, tab_recv.at[1])
                for f in fetch:
                    f.start()
            if tick < len(arrivals):
                for j in arrivals[tick]:
                    if j:
                        c1_wait(j)
                    for to in onwards.get(j, ()):
                        c1_copy(j, to).start()
            for phase in range(5):
                if 0 <= tick - phase < len(arrivals):
                    for j in arrivals[tick - phase]:
                        plane_step(j, phase)
        own_copy().wait()

        choose(lambda s: pairs_ref[0, s], count_ref[0, 0])

        def own_step(k, carry):
            h_own[k], h_own[quarter + k] = half(t_own, k)
            return carry
        lax.fori_loop(0, quarter, own_step, 0)
        for f in fetch:
            f.wait()
        arrived(t_side, side_recv)
        choose(lambda s: tabs[0, 0, s], tabs[0, 0, slots])

        def side_step(k, carry):
            h_side[k], h_side[quarter + k] = half(t_side, k)
            return carry
        lax.fori_loop(0, quarter, side_step, 0)
        choose(lambda s: tabs[1, 0, s], tabs[1, 0, slots])

        if high:
            arrived(t_cross.at[:, pl.ds(low, high)], high_recv)

        def cross_step(k, carry):
            for p in (k, quarter + k):
                arrived(t_cross.at[p, pl.ds(0, low)], cross_recv.at[p])
            for p, h_cross in zip((k, quarter + k), half(t_cross, k)):
                both = jnp.concatenate([h_own[p], h_cross], axis=0)
                gram[...] += nt(both, both)
                side[...] += nt(h_cross, h_side[p])
            return carry
        lax.fori_loop(0, quarter, cross_step, 0)

        def cut(block):
            return block.reshape(stage_b.shape)

        @pl.when(hi == 0)
        def _():
            stage_a[:, 0] = cut(gram[:bs, :bs])
            stage_a[:, 1] = cut(gram[:bs, bs:])
            stage_b[...] = cut(gram[bs:, bs:])
            stage_c[...] = cut(side[...])

        @pl.when(hi == 1)
        def _():
            stage_a[:, 0] = cut(gram[bs:, bs:])
            stage_a[:, 1] = cut(gram[bs:, :bs])
            stage_b[...] = cut(gram[:bs, :bs])
            stage_c[...] = cut(side[...].T)

        for i in range(HALF):
            away_a = jnp.logical_or(zlo != i, hi == 1)
            away_b = jnp.logical_or(zlo != i, hi == 0)

            @pl.when(away_a)
            def _():
                part_a(i).start()

            @pl.when(jnp.logical_not(away_a))
            def _():
                pltpu.make_async_copy(stage_a.at[i], parts.at[g], part_recv).start()

            @pl.when(away_b)
            def _():
                part_b(i).start()

            @pl.when(jnp.logical_not(away_b))
            def _():
                pltpu.make_async_copy(stage_b.at[i], parts.at[g, 0], part_recv).start()
            part_c(i).start()

        arrived(parts, part_recv)
        total[...] = jnp.sum(parts[...], axis=0) * factor
        total_copy().start()
        if high:
            arrived(over, over_recv)
            over_ref[...] = over[...]
        mine = total[:, pl.ds(pl.multiple_of(hi * rows, rows), rows)]
        diag_ref[0] = mine[0]
        next_ref[0] = mine[1]

        total_copy().wait_send()
        tab_copy(0).wait_send()
        tab_copy(1).wait_send()
        side_copy().wait_send()
        beside_copy().wait_send()
        for j, tos in onwards.items():
            for to in tos:
                c1_copy(j, to).wait_send()
        for units in arrivals:
            for j in units:
                arrived(c_all.at[pl.ds(0, NY + 1), pl.ds(0, NX - 1), 0, pl.ds(0, 2)], plane_send.at[j + 4])

        @pl.when(hi == 0)
        def _():
            arrived(parts.at[pl.ds(0, HALF - 1)], part_send.at[0])
            arrived(parts.at[pl.ds(0, HALF // 2)], part_send.at[1])

        @pl.when(hi == 1)
        def _():
            arrived(parts.at[pl.ds(0, HALF)], part_send.at[0])
            arrived(parts.at[pl.ds(0, HALF - 1), 0], part_send.at[1])
        arrived(parts.at[pl.ds(0, HALF // 2)], part_send.at[2])


def run(low, room, collective_id, three_centre, occupied_coefficients, paired_blocks, stored_counts):
    naux, _, slots, bs, _ = three_centre.shape
    groups = HALF * CORES
    cols = occupied_coefficients.shape[1]
    nocc = cols * groups
    factor = 1.0 / math.sqrt(naux * groups * nocc)
    rows = bs // groups
    dma = pltpu.SemaphoreType.DMA
    vmem = pl.BlockSpec(memory_space=pltpu.VMEM)
    smem = pl.BlockSpec(memory_space=pltpu.SMEM)
    slab = (naux, slots, bs, bs)
    strip = bs * naux // RINGS
    high, room = max(slots - low, 1), max(room, 1)
    tile = jax.ShapeDtypeStruct((1, 128), jnp.int32)
    return pl.pallas_call(
        functools.partial(kernel, factor, low, room),
        out_shape=[jax.ShapeDtypeStruct((1, rows, bs), F32)] * 2 + [tile],
        in_specs=[smem, smem, vmem, pl.BlockSpec(memory_space=pl.ANY)],
        out_specs=[vmem, vmem, vmem],
        scratch_shapes=[
            pltpu.VMEM((RINGS, high, strip, bs), BF16),
            pltpu.VMEM((room, strip, bs), BF16),
            pltpu.VMEM((room, strip, bs), BF16),
            pltpu.VMEM((room, strip, bs), BF16),
            pltpu.VMEM((RINGS, high, strip, bs), BF16),
            pltpu.VMEM((RINGS, 1, 128), jnp.int32),
            pltpu.VMEM((1, 128), jnp.int32),
            pltpu.VMEM((1, 128), jnp.int32),
            pltpu.SMEM((1, 128), jnp.int32),
            pltpu.SMEM((1, 128), jnp.int32),
            pltpu.SMEM((RINGS,), jnp.int32),
            dma, dma, dma, dma, dma, dma, dma, dma,
            dma((2,)), dma((2,)), dma((2,)), dma((2,)), dma, dma, dma,
            pltpu.VMEM((2 * cols, bs), BF16),
            pltpu.VMEM((NY + 1, NX, 2, HALF, bs, bs), BF16),
            pltpu.VMEM(slab, BF16),
            pltpu.VMEM(slab, BF16),
            pltpu.VMEM(slab, BF16),
            pltpu.VMEM((naux, low, bs, bs), BF16),
            pltpu.VMEM((slots * bs, nocc), BF16),
            pltpu.VMEM((naux, bs, nocc), BF16),
            pltpu.VMEM((naux, bs, nocc), BF16),
            pltpu.VMEM((2 * bs, 2 * bs), F32),
            pltpu.VMEM((bs, bs), F32),
            pltpu.VMEM((HALF, 2, 2 * rows, bs), F32),
            pltpu.VMEM((HALF, 2 * rows, bs), F32),
            pltpu.VMEM((HALF, 2 * rows, bs), F32),
            pltpu.VMEM((groups, 2, 2 * rows, bs), F32),
            pltpu.VMEM((2, 2 * rows, bs), F32),
            pltpu.VMEM((1, 128), jnp.int32),
            pltpu.VMEM((1, 128), jnp.int32),
            pltpu.VMEM((1, 128), jnp.int32),
            pltpu.SMEM((2, 1, 128), jnp.int32),
            dma, dma, dma, dma, dma((NZ // 2,)), dma((NZ // 2,)), dma((NZ // 2,)), dma((NZ // 2, 2, 4)),
            dma((naux,)), dma((naux,)), dma((naux,)), dma((naux,)), dma, dma,
            dma((2,)), dma((2,)), dma, dma((2,)), dma((3,)), dma, dma, dma,
            pltpu.SemaphoreType.REGULAR,
        ],
        compiler_params=pltpu.CompilerParams(
            collective_id=collective_id, has_side_effects=True, vmem_limit_bytes=60 * 1024 * 1024),
        cost_estimate=pl.CostEstimate(flops=8 * 10**9, bytes_accessed=6 * 2**20, transcendentals=0),
    )(paired_blocks, stored_counts[None], occupied_coefficients.T, three_centre)


def body(*args):
    slots = args[0].shape[2]
    diag, following, over = run(STILL, ROOM, 0, *args)
    return lax.cond(over[0, 0] > 0, lambda: tuple(run(slots, 0, 1, *args)[:2]), lambda: (diag, following))


def solution(mesh):
    placed = (P("grp", "blk", None, None, None), P("blk", "grp"), P("blk", None), P("blk"))
    return jax.shard_map(
        body,
        mesh=mesh,
        in_specs=placed,
        out_specs=(P("blk", "grp", None), P("blk", "grp", None)),
        check_vma=False,
    )
```
